128 devices in a mesh: row: 16 (over x, z), col: 8 (over y, core).
Axes of the slice: x: 4, y: 4, z: 4, core: 2. Of those that a mesh axis runs over, the one named last changes fastest.
Arguments:
- object_field: float32 [2, 8192, 3072], P(None, 'row', 'col'), may hold values from -6 to 6
- probe_field: float32 [2, 256, 256], replicated, may hold values from -6 to 6
- amplitudes: bfloat16 [2, 1536, 256, 256], P(None, ('row', 'col')), may hold values from 0.29882812 to 3
- positions: int32 [2, 2, 1536], P(None, None, ('row', 'col')), may hold values from 0 to 511, as said below
- live_counts: int32 [2, 8, 16], P(None, 'col', 'row'), may hold values from 1 to 12, 48 in all within a row
Outputs:
- object_out: float32 [2, 8192, 3072], P(None, 'row', 'col')
- probe_out: float32 [2, 256, 256], replicated
The draws below stay inside these ranges and needn't reach their ends.
Inputs may be any that keep to these rules, and one draw needn't show every extreme that they name: `positions`: every offset is below 512 for rows and below 384 for columns; in the last block row the row offset is at most 256, in the last block column the column offset at most 128, so every patch lies inside the object. The live frames of a device are its first slots. For every iteration t and block column c, the 16 counts live_counts[t, c, :] of that block column's devices sum to 48, and one of them is 12; no such sum holds over the devices of a block row.
All inputs are finite; a program needn't handle non-finite values.
Results may differ from the reference program's by a relative error of at most 0.0019.
Values may be sent and summed in bfloat16 or wider, within the bound.
No kernel may reach another device: no remote copies, remote signals or barrier semaphores. Data moves between devices by JAX's collectives and lax.ppermute only.
A program may use at most 128 MiB of HBM per device.

```python
import math
import jax
import jax.numpy as jnp
import numpy as np
from jax import lax

FRAME = 256
TILE_ROWS = 512
TILE_COLS = 384
BATCH_DEV = 3
ITERS = 2
FRAMES_DEV = 12
FRAMES = 1536
ROWS = 8192
COLS = 3072
N_ROW = 16
N_COL = 8
DEVICES = 128


def draw_positions(key, part):
    frame_ids = jnp.arange(FRAMES, dtype=jnp.int32)
    device_ids = frame_ids // FRAMES_DEV
    row_ids = device_ids // N_COL
    col_ids = device_ids % N_COL
    row_high = jnp.where(row_ids == N_ROW - 1, TILE_ROWS - FRAME + 1, TILE_ROWS).astype(jnp.int32)
    col_high = jnp.where(col_ids == N_COL - 1, TILE_COLS - FRAME + 1, TILE_COLS).astype(jnp.int32)
    key_rows = jax.random.fold_in(key, 11)
    key_columns = jax.random.fold_in(key, 23)
    row_draw = jax.random.randint(key_rows, (ITERS, FRAMES), 0, row_high[None, :], dtype=jnp.int32)
    col_draw = jax.random.randint(key_columns, (ITERS, FRAMES), 0, col_high[None, :], dtype=jnp.int32)
    return jnp.stack([row_draw, col_draw], axis=1)


def block_levels(rng, extent, pieces, least, top_value):
    def one(dim, blocks):
        draws = jax.random.uniform(jax.random.fold_in(jax.random.fold_in(rng, 6), dim), (blocks,), jnp.float32, least / len(pieces), top_value / len(pieces))
        return jnp.repeat(jnp.exp(draws), extent[dim] // blocks).reshape((-1,) + (1,) * (len(extent) - dim - 1))

    level = one(*pieces[0])
    for cut in pieces[1:]:
        level = level * one(*cut)
    return level


def split_up(count, total, reach, slope):
    weights = [(1 << 20) // math.isqrt(standing ** slope) + 1 for standing in range(2, count + 1)]
    spare, holding = total - reach - (count - 1), [1] * (count - 1)
    while spare > 0:
        movable = [i for i in range(count - 1) if holding[i] < reach]
        mass, budget = sum([weights[i] for i in movable]), spare
        for i in movable:
            extra = min(reach - holding[i], max(1, budget * weights[i] // mass), spare)
            holding[i] = holding[i] + extra
            spare = spare - extra
    return np.array([reach] + holding)


def uneven_parts(key, number_of, total, limit, skew):
    if number_of == 2:
        one = jax.random.randint(key, (), max(1, total - limit), min(limit, total - 1) + 1)
        return jnp.stack([one, total - one])
    sizes = jnp.asarray(split_up(number_of, total, limit, skew), jnp.int32)
    twos = (number_of - 1) // 2
    giver, receiver = sizes[1:1 + 2 * twos:2], sizes[2:2 + 2 * twos:2]
    slack = jnp.minimum(giver - 1, limit - receiver)
    passed = jax.random.randint(jax.random.fold_in(key, 1), (twos,), 0, 1 << 20) % (slack + 1)
    sizes = sizes.at[1:1 + 2 * twos:2].set(giver - passed).at[2:2 + 2 * twos:2].set(receiver + passed)
    return sizes[jax.random.permutation(jax.random.fold_in(key, 2), number_of)]


def scatter_about(own_key, extent, scale, bound, cuts=(), kind=jnp.bfloat16):
    level = block_levels(own_key, extent, cuts, -0.22, 0.18) if cuts else 1.0
    array = jax.random.normal(own_key, extent, jnp.float32) * scale * level
    return jnp.minimum(jnp.maximum(array, -bound), bound).astype(kind)


def setup_inputs(seed: int = 0) -> dict:
    key_list = jax.random.split(jax.random.key(seed), 6)
    return {
        "object_field": scatter_about(key_list[0], (2, ROWS, COLS), 1.0, 6.0, ((1, 16), (2, 8)), jnp.float32),
        "probe_field": scatter_about(key_list[1], (2, FRAME, FRAME), 1.0, 6.0, (), jnp.float32),
        "amplitudes": jnp.clip(jnp.exp(math.log(3.0) - 2.306499 * jax.random.uniform(key_list[2], (ITERS, FRAMES, FRAME, FRAME), jnp.float32) ** block_levels(key_list[2], (ITERS, FRAMES, FRAME, FRAME), ((1, 128),), -0.2, 0.2)), 0.29882812, 3.0).astype(jnp.bfloat16),
        "positions": draw_positions(jax.random.fold_in(key_list[5], 71), 0),
        "live_counts": jax.vmap(lambda own: uneven_parts(own, N_ROW, N_ROW * BATCH_DEV, FRAMES_DEV, 2))(jax.random.split(key_list[4], ITERS * N_COL)).reshape((ITERS, N_COL, N_ROW)).astype(jnp.int32),
    }


FLOOR = 0.3
ALPHA = 0.5

def chirp_tables(frame_size):
    offset = jnp.arange(frame_size, dtype=jnp.int32)
    differ = offset[:, None] - offset[None, :]
    phase_units = differ * differ % (2 * frame_size)
    phase = jnp.pi * phase_units.astype(jnp.float32) / frame_size
    scale = 1.0 / math.sqrt(frame_size)
    return ((jnp.cos(phase) * scale).astype(jnp.bfloat16), (jnp.sin(phase) * scale).astype(jnp.bfloat16))

def left_product(real_table, imag_table, real_part, imag_part):

    def product(table, part):
        return jnp.einsum('ab,nbc->nac', table.astype(jnp.float32), part.astype(jnp.float32))
    return (product(real_table, real_part) - product(imag_table, imag_part), product(real_table, imag_part) + product(imag_table, real_part))

def right_product(real_table, imag_table, real_part, imag_part):

    def product(part, table):
        return jnp.einsum('nab,bc->nac', part.astype(jnp.float32), table.astype(jnp.float32))
    return (product(real_part, real_table) - product(imag_part, imag_table), product(imag_part, real_table) + product(real_part, imag_table))

def frame_terms(patches, frame_amps, probe_field, real_table, imag_table, weights):
    probe_real, probe_imag = (probe_field[0], probe_field[1])
    patch_real = patches[:, 0].astype(jnp.float32)
    patch_imag = patches[:, 1].astype(jnp.float32)
    wave_real = (probe_real * patch_real - probe_imag * patch_imag).astype(jnp.bfloat16)
    wave_imag = (probe_real * patch_imag + probe_imag * patch_real).astype(jnp.bfloat16)
    near_real, near_imag = left_product(real_table, imag_table, wave_real, wave_imag)
    near_real, near_imag = (near_real.astype(jnp.bfloat16), near_imag.astype(jnp.bfloat16))
    far_real, far_imag = right_product(real_table, imag_table, near_real, near_imag)
    magnitude = jnp.sqrt(far_real * far_real + far_imag * far_imag)
    factor = 1.0 - frame_amps.astype(jnp.float32) / jnp.maximum(magnitude, FLOOR)
    misfit_real = (far_real * factor).astype(jnp.bfloat16)
    misfit_imag = (far_imag * factor).astype(jnp.bfloat16)
    conj_table = -imag_table
    back_real, back_imag = left_product(real_table, conj_table, misfit_real, misfit_imag)
    back_real, back_imag = (back_real.astype(jnp.bfloat16), back_imag.astype(jnp.bfloat16))
    update_real, update_imag = right_product(real_table, conj_table, back_real, back_imag)
    weight_col = weights[:, None, None]
    grad_real = (probe_real * update_real + probe_imag * update_imag) * weight_col
    grad_imag = (probe_real * update_imag - probe_imag * update_real) * weight_col
    gradients = jnp.stack([grad_real, grad_imag], axis=1).astype(jnp.bfloat16)
    probe_real_term = lax.optimization_barrier(jnp.sum(weight_col * (patch_real * update_real + patch_imag * update_imag), axis=0))
    probe_imag_term = lax.optimization_barrier(jnp.sum(weight_col * (patch_real * update_imag - patch_imag * update_real), axis=0))
    weight_term = lax.optimization_barrier(jnp.sum(weight_col * (patch_real * patch_real + patch_imag * patch_imag), axis=0))
    return (gradients, jnp.stack([probe_real_term, probe_imag_term], axis=0), weight_term)

def reference(object_field, probe_field, amplitudes, positions, live_counts):
    real_table, imag_table = chirp_tables(FRAME)
    frame_ids = jnp.arange(FRAMES, dtype=jnp.int32)
    device_ids = frame_ids // FRAMES_DEV
    slot_ids = frame_ids % FRAMES_DEV
    row_ids = device_ids // N_COL
    col_ids = device_ids % N_COL
    anchor = jnp.zeros((), jnp.int32)
    live_total = DEVICES * BATCH_DEV
    for iteration in range(ITERS):
        counts = live_counts[iteration][col_ids, row_ids]
        chosen = jnp.nonzero(slot_ids < counts, size=live_total)[0].astype(jnp.int32)
        top_rows = (row_ids[chosen] * TILE_ROWS + positions[iteration, 0][chosen]).astype(jnp.int32)
        left_columns = (col_ids[chosen] * TILE_COLS + positions[iteration, 1][chosen]).astype(jnp.int32)
        chosen_amps = amplitudes[iteration][chosen]

        def block_terms(block):
            block_tops, block_lefts, block_amps = block

            def cut_patch(top_row, left_column):
                return lax.dynamic_slice(object_field, (anchor, top_row, left_column), (2, FRAME, FRAME))
            patches = jax.vmap(cut_patch)(block_tops, block_lefts).astype(jnp.bfloat16)
            return frame_terms(patches, block_amps, probe_field, real_table, imag_table, jnp.ones((BATCH_DEV,), jnp.float32))
        gradients, probe_terms, weight_terms = lax.map(block_terms, (top_rows.reshape(DEVICES, BATCH_DEV), left_columns.reshape(DEVICES, BATCH_DEV), chosen_amps.reshape(DEVICES, BATCH_DEV, FRAME, FRAME)))
        flat_grads = gradients.reshape(live_total, 2, FRAME, FRAME)

        def add_patch(index, total):
            corner = (anchor, top_rows[index], left_columns[index])
            current = lax.dynamic_slice(total, corner, (2, FRAME, FRAME))
            return lax.dynamic_update_slice(total, current + flat_grads[index].astype(jnp.float32), corner)
        object_sum = lax.fori_loop(0, live_total, add_patch, jnp.zeros_like(object_field))
        probe_sum = lax.optimization_barrier(jnp.sum(probe_terms, axis=0))
        weight_sum = lax.optimization_barrier(jnp.sum(weight_terms, axis=0))
        step_size = ALPHA / (jnp.max(probe_field[0] * probe_field[0] + probe_field[1] * probe_field[1]) + 1e-06)
        object_field = object_field - step_size * object_sum
        probe_field = probe_field - probe_sum / (weight_sum + 1.0)
    return (object_field, probe_field)
```

```python
import functools

import jax
import jax.numpy as jnp
import ml_dtypes
import numpy as np
from jax import lax
from jax.experimental import pallas as pl
from jax.experimental.pallas import tpu as pltpu
from jax.sharding import Mesh, PartitionSpec as P

ITERS = 2
FLOOR = 0.3
ALPHA = 0.5
LANES = 128
CHUNK = 32
N_X, N_Z, N_Y, N_CORE = 4, 4, 4, 2
N_ROW, N_COL = N_X * N_Z, N_Y * N_CORE
ROW, COL = ("x", "z"), ("y", "core")
BF, F32 = jnp.bfloat16, jnp.float32


def chirp_blocks(size):
    offset = np.arange(size, dtype=np.int64)
    units = (offset[:, None] - offset[None, :]) ** 2 % (2 * size)
    phase = np.float32(np.pi) * units.astype(np.float32) / np.float32(size)
    scale = np.float32(1.0 / np.sqrt(size))
    real = (np.cos(phase) * scale).astype(ml_dtypes.bfloat16)
    imag = (np.sin(phase) * scale).astype(ml_dtypes.bfloat16)
    forward = np.block([[real, -imag], [imag, real]])
    return forward, np.ascontiguousarray(forward.T)


def frames_kernel(
    place, counts, pos,
    obj, below, right, corner, probe, amps, table_a, table_b,
    own_out, below_out, right_out, corner_out, keep_out, send_out, step_out,
    ext, acc, sums, wave, mis, patch,
):
    rows, cols = obj.shape[1], obj.shape[2]
    size = probe.shape[1]
    row_chunks = size // CHUNK
    inner_tiles, all_tiles = cols // LANES, (cols + size) // LANES
    for j in range(all_tiles):
        upper, lower = (obj, below) if j < inner_tiles else (right, corner)
        at = (j if j < inner_tiles else j - inner_tiles) * LANES
        ext[:, j, :rows, :] = upper[:, :, at : at + LANES].astype(BF).astype(F32)
        ext[:, j, rows:, :] = lower[:, :, at : at + LANES].astype(F32)
    acc[...] = jnp.zeros_like(acc)
    sums[...] = jnp.zeros_like(sums)
    peak = jnp.max(probe[0] * probe[0] + probe[1] * probe[1])
    step_out[0, 0] = ALPHA / (peak + 1e-6)
    lane = lax.broadcasted_iota(jnp.int32, (CHUNK, LANES), 1)

    def frame(index, carry):
        top, left = pos[0, index], pos[1, index]
        base = left // LANES
        shift = left - base * LANES
        back_shift = lax.rem(LANES - shift, LANES)
        whole = lane < LANES - shift
        fresh = lane >= shift
        for k in range(row_chunks):
            span = slice(k * CHUNK, (k + 1) * CHUNK)
            parts = []
            for c in range(2):
                tiles = [
                    pltpu.roll(ext[c, base + j, pl.ds(top + k * CHUNK, CHUNK), :], back_shift, 1)
                    for j in range(3)
                ]
                cut = jnp.concatenate(
                    [jnp.where(whole, tiles[0], tiles[1]), jnp.where(whole, tiles[1], tiles[2])], axis=1
                )
                patch[c, span, :] = cut
                parts.append(cut)
            re, im = parts
            pr, pi = probe[0, span, :], probe[1, span, :]
            wave[span, :] = (pr * re - pi * im).astype(BF)
            wave[size + k * CHUNK : size + (k + 1) * CHUNK, :] = (pr * im + pi * re).astype(BF)
            sums[2, span, :] += re * re + im * im
        near = jnp.dot(table_a[...], wave[...], preferred_element_type=F32).astype(BF)
        near = jnp.concatenate([near[:size], near[size:]], axis=1)
        far = jnp.dot(near, table_b[...], preferred_element_type=F32)
        fr, fi = far[:, :size], far[:, size:]
        scale = lax.rsqrt(jnp.maximum(fr * fr + fi * fi, FLOOR * FLOOR))
        factor = 1.0 - amps[0, index].astype(F32) * scale
        mis[:size, :] = (fr * factor).astype(BF)
        mis[size:, :] = (fi * factor).astype(BF)
        back = jnp.dot(table_b[...], mis[...], preferred_element_type=F32).astype(BF)
        back = jnp.concatenate([back[:size], back[size:]], axis=1)
        update = jnp.dot(back, table_a[...], preferred_element_type=F32)
        for k in range(row_chunks):
            span = slice(k * CHUNK, (k + 1) * CHUNK)
            ur, ui = update[span, :size], update[span, size:]
            pr, pi = probe[0, span, :], probe[1, span, :]
            re, im = patch[0, span, :], patch[1, span, :]
            sums[0, span, :] += re * ur + im * ui
            sums[1, span, :] += re * ui - im * ur
            grads = (pr * ur + pi * ui, pr * ui - pi * ur)
            for c in range(2):
                grad = grads[c].astype(BF).astype(F32)
                first = pltpu.roll(grad[:, :LANES], shift, 1)
                second = pltpu.roll(grad[:, LANES:], shift, 1)
                pieces = (
                    jnp.where(fresh, first, 0.0),
                    jnp.where(fresh, second, first),
                    jnp.where(fresh, 0.0, second),
                )
                for j, piece in enumerate(pieces):
                    acc[c, base + j, pl.ds(top + k * CHUNK, CHUNK), :] += piece
        return carry

    lax.fori_loop(0, counts[0], frame, 0)
    for j in range(all_tiles):
        upper, lower = (own_out, below_out) if j < inner_tiles else (right_out, corner_out)
        at = (j if j < inner_tiles else j - inner_tiles) * LANES
        upper[:, :, at : at + LANES] = acc[:, j, :rows, :].astype(upper.dtype)
        lower[:, :, at : at + LANES] = acc[:, j, rows:, :].astype(BF)
    core, y = place[0], place[1]
    half, quarter = size // N_CORE, size // (N_CORE * N_Y)
    for j in range(N_Y):
        inner = lax.rem(y + j, N_Y) * quarter
        keep_at = pl.multiple_of(core * half + inner, quarter)
        send_at = pl.multiple_of((1 - core) * half + inner, quarter)
        keep_out[j] = sums[:, pl.ds(keep_at, quarter), :]
        send_out[j] = sums[:, pl.ds(send_at, quarter), :]


def run_frames(place, counts, pos, obj, halos, probe, amps, tables, iteration):
    rows, cols = obj.shape[1], obj.shape[2]
    size = probe.shape[1]
    slots = amps.shape[1]
    vmem = pl.BlockSpec(memory_space=pltpu.VMEM)
    smem = pl.BlockSpec(memory_space=pltpu.SMEM)
    quarter = size // (N_CORE * N_Y)
    shapes = [
        jax.ShapeDtypeStruct((2, rows, cols), F32),
        jax.ShapeDtypeStruct((2, size, cols), BF),
        jax.ShapeDtypeStruct((2, rows, size), BF),
        jax.ShapeDtypeStruct((2, size, size), BF),
        jax.ShapeDtypeStruct((N_Y, 3, quarter, size), F32),
        jax.ShapeDtypeStruct((N_Y, 3, quarter, size), F32),
        jax.ShapeDtypeStruct((1, 1), F32),
    ]
    amp_spec = pl.BlockSpec((1, slots, size, size), lambda i: (iteration, 0, 0, 0))
    return pl.pallas_call(
        frames_kernel,
        grid=(1,),
        out_shape=shapes,
        in_specs=[smem] * 3 + [vmem] * 5 + [amp_spec] + [vmem] * 2,
        out_specs=[vmem] * 6 + [smem],
        scratch_shapes=[
            pltpu.VMEM((2, (cols + size) // LANES, rows + size, LANES), F32),
            pltpu.VMEM((2, (cols + size) // LANES, rows + size, LANES), F32),
            pltpu.VMEM((3, size, size), F32),
            pltpu.VMEM((2 * size, size), BF),
            pltpu.VMEM((2 * size, size), BF),
            pltpu.VMEM((2, size, size), F32),
        ],
        compiler_params=pltpu.CompilerParams(vmem_limit_bytes=48 << 20),
        cost_estimate=pl.CostEstimate(flops=6_000_000_000, bytes_accessed=8_000_000, transcendentals=0),
        name="frames",
    )(place, counts, pos, obj, *halos, probe, amps, *tables)


def update_kernel(obj, own, above, left, diag, step, obj_out, below_out, right_out):
    size = left.shape[2]
    rows = obj.shape[1]
    alpha = step[0, 0]
    rest_cols = obj.shape[2] - size
    a, l, d = above[...].astype(F32), left[...].astype(F32), diag[...].astype(F32)
    obj_out[:, :size, :size] = obj[:, :size, :size] - alpha * (
        own[:, :size, :size] + l[:, :size] + a[:, :, :size] + d
    )
    obj_out[:, :size, size:] = obj[:, :size, size:] - alpha * (own[:, :size, size:] + a[:, :, size:])
    obj_out[:, size:, :size] = obj[:, size:, :size] - alpha * (own[:, size:, :size] + l[:, size:])
    obj_out[:, size:, size:] = obj[:, size:, size:] - alpha * own[:, size:, size:]
    below_out[...] = obj_out[:, :size, :].astype(BF)
    right_out[...] = obj_out[:, :, :size].astype(BF)


def run_update(obj, own, above, left, diag, step):
    rows, cols = obj.shape[1], obj.shape[2]
    size = left.shape[2]
    vmem = pl.BlockSpec(memory_space=pltpu.VMEM)
    smem = pl.BlockSpec(memory_space=pltpu.SMEM)
    return pl.pallas_call(
        update_kernel,
        out_shape=[
            jax.ShapeDtypeStruct((2, rows, cols), F32),
            jax.ShapeDtypeStruct((2, size, cols), BF),
            jax.ShapeDtypeStruct((2, rows, size), BF),
        ],
        in_specs=[vmem] * 5 + [smem],
        out_specs=[vmem] * 3,
        compiler_params=pltpu.CompilerParams(vmem_limit_bytes=32 << 20),
        cost_estimate=pl.CostEstimate(flops=2_000_000, bytes_accessed=8_000_000, transcendentals=0),
        name="object_update",
    )(obj, own, above, left, diag, step)


def moved(value, axis, count, steps):
    first, last = max(0, -steps), min(count, count - steps)
    return lax.ppermute(value, axis, [(s, s + steps) for s in range(first, last)])


def moved_both(value, steps):
    pairs = []
    for r in range(N_ROW):
        for c in range(N_COL):
            to_r, to_c = r + steps, c + steps
            if 0 <= to_r < N_ROW and 0 <= to_c < N_COL:
                pairs.append((r * N_COL + c, to_r * N_COL + to_c))
    return lax.ppermute(value, ROW + COL, pairs)


def turned(value, axis, steps):
    return lax.ppermute(value, axis, [(s, (s + steps) % 4) for s in range(4)])


def swapped(value):
    return lax.ppermute(value, "core", [(0, 1), (1, 0)])


def halo(below, right, size):
    return (
        moved(below, ROW, N_ROW, -1),
        moved(right, COL, N_COL, -1),
        moved_both(below[:, :, :size], -1),
    )


def new_probe(keep, send, probe, place):
    size = probe.shape[1]
    half, quarter = size // N_CORE, size // (N_CORE * N_Y)
    core, y = place[0], place[1]
    part = keep + swapped(send)
    total = part[0]
    for j in range(1, N_Y):
        total = total + turned(part[j], "y", j)
    for axis in ("z", "x"):
        total = total + turned(total, axis, 1) + turned(total, axis, 2) + turned(total, axis, 3)
    mine = lax.dynamic_slice(probe, (0, core * half + y * quarter, 0), (2, quarter, size))
    fresh = mine - total[:2] / (total[2] + 1.0)
    chunks = [fresh] + [turned(fresh, "y", j) for j in range(1, N_Y)]
    mine_half = jnp.concatenate(chunks[::-1] + chunks[::-1], axis=1)
    at = lax.rem(N_Y - 1 - y + N_Y, N_Y) * quarter
    mine_half = lax.dynamic_slice(mine_half, (0, at, 0), (2, half, size))
    other = swapped(mine_half)
    first = jnp.where(core == 0, mine_half, other)
    second = jnp.where(core == 0, other, mine_half)
    return jnp.concatenate([first, second], axis=1)


def local(tables, obj, probe, amps, positions, counts):
    size = probe.shape[-1]
    place = jnp.stack([lax.axis_index("core"), lax.axis_index("y")]).astype(jnp.int32)
    below, right = obj[:, :size, :].astype(BF), obj[:, :, :size].astype(BF)
    for iteration in range(ITERS):
        halos = halo(below, right, size)
        own, down, across, both, keep, send, step = run_frames(
            place, counts[iteration, 0], positions[iteration], obj, halos, probe, amps, tables, iteration
        )
        diag = moved_both(both, 1)
        left = moved(across, COL, N_COL, 1)
        above = moved(down, ROW, N_ROW, 1)
        probe = new_probe(keep, send, probe, place)
        obj, below, right = run_update(obj, own, above, left, diag, step)
    return (obj, probe)


def solution(mesh):
    fine = Mesh(mesh.devices.reshape(N_X, N_Z, N_Y, N_CORE), ("x", "z", "y", "core"))
    placed = (
        P(None, ROW, COL),
        P(),
        P(None, ROW + COL, None, None),
        P(None, None, ROW + COL),
        P(None, COL, ROW),
    )
    blocks = tuple(jnp.asarray(block) for block in chirp_blocks(256))
    return jax.shard_map(
        functools.partial(local, blocks),
        mesh=fine, in_specs=placed, out_specs=(P(None, ROW, COL), P()), check_vma=False,
    )
```

```python
import functools

import jax
import jax.numpy as jnp
import ml_dtypes
import numpy as np
from jax import lax
from jax.experimental import pallas as pl
from jax.experimental.pallas import tpu as pltpu
from jax.sharding import Mesh, PartitionSpec as P

ITERS = 2
FLOOR = 0.3
ALPHA = 0.5
LANES = 128
CHUNK = 32
GROUPS = (4, 2, 1)
N_X, N_Z, N_Y, N_CORE = 4, 4, 4, 2
N_ROW, N_COL = N_X * N_Z, N_Y * N_CORE
ROW, COL = ("x", "z"), ("y", "core")
BF, F32 = jnp.bfloat16, jnp.float32


def chirp_blocks(size):
    offset = np.arange(size, dtype=np.int64)
    units = (offset[:, None] - offset[None, :]) ** 2 % (2 * size)
    phase = np.float32(np.pi) * units.astype(np.float32) / np.float32(size)
    scale = np.float32(1.0 / np.sqrt(size))
    real = (np.cos(phase) * scale).astype(ml_dtypes.bfloat16)
    imag = (np.sin(phase) * scale).astype(ml_dtypes.bfloat16)
    forward = np.block([[real, -imag], [imag, real]])
    return forward, np.ascontiguousarray(forward.T)


def frames_kernel(
    iteration, n_pieces,
    place, counts, pos, obj, below_left, below_right, right, corner, *rest,
):
    pieces, (amps, table_a, table_b), rest = rest[:n_pieces], rest[n_pieces : n_pieces + 3], rest[n_pieces + 3 :]
    own_out, low_left, low_right, right_out, corner_out, keep_out, send_out, step_out = rest[:8]
    ext, acc, sums, wave, mis, patch, levels, arrived, *probe_scratch = rest[8:]
    count = counts[0]

    def fetch(index):
        return pltpu.make_async_copy(amps.at[iteration, index], levels.at[index], arrived.at[index])

    def begin(index, carry):
        fetch(index).start()
        return carry

    lax.fori_loop(0, count, begin, 0)
    rows, cols = obj.shape[1], obj.shape[2]
    size = corner.shape[1]
    core, y = place[0], place[1]
    half, quarter = size // N_CORE, size // (N_CORE * N_Y)
    if n_pieces == 1:
        (probe,) = pieces
    else:
        (probe,) = probe_scratch
        for piece, side in ((pieces[0], core), (pieces[1], 1 - core)):
            for j in range(N_Y):
                at = pl.multiple_of(side * half + lax.rem(y - j + N_Y, N_Y) * quarter, quarter)
                probe[:, pl.ds(at, quarter), :] = piece[j]
    row_chunks = size // CHUNK
    inner_tiles, all_tiles, left_tiles = cols // LANES, (cols + size) // LANES, size // LANES
    for j in range(all_tiles):
        inside = j < inner_tiles
        at = (j if inside else j - inner_tiles) * LANES
        upper = obj if inside else right
        ext[:, j, :rows, :] = upper[:, :, at : at + LANES].astype(BF).astype(F32)
        lower = (below_left if j < left_tiles else below_right) if inside else corner
        at = at if j < left_tiles or not inside else at - size
        ext[:, j, rows:, :] = lower[:, :, at : at + LANES].astype(F32)
    acc[...] = jnp.zeros_like(acc)
    sums[...] = jnp.zeros_like(sums)
    peak = jnp.max(probe[0] * probe[0] + probe[1] * probe[1])
    step_out[0, 0] = ALPHA / (peak + 1e-6)
    lane = lax.broadcasted_iota(jnp.int32, (CHUNK, LANES), 1)

    def frames(indices):
        work = []
        for slot, index in enumerate(indices):
            top, left = pos[0, index], pos[1, index]
            base = left // LANES
            shift = left - base * LANES
            back_shift = lax.rem(LANES - shift, LANES)
            whole = lane < LANES - shift
            for k in range(row_chunks):
                span = slice(k * CHUNK, (k + 1) * CHUNK)
                parts = []
                for c in range(2):
                    tiles = [
                        pltpu.roll(ext[c, base + j, pl.ds(top + k * CHUNK, CHUNK), :], back_shift, 1)
                        for j in range(3)
                    ]
                    cut = jnp.concatenate(
                        [jnp.where(whole, tiles[0], tiles[1]), jnp.where(whole, tiles[1], tiles[2])], axis=1
                    )
                    patch[slot, c, span, :] = cut
                    parts.append(cut)
                re, im = parts
                pr, pi = probe[0, span, :], probe[1, span, :]
                wave[slot, span, :] = (pr * re - pi * im).astype(BF)
                wave[slot, size + k * CHUNK : size + (k + 1) * CHUNK, :] = (pr * im + pi * re).astype(BF)
                sums[2, span, :] += re * re + im * im
            work.append((index, top, base, shift))
        for slot, (index, top, base, shift) in enumerate(work):
            near = jnp.dot(table_a[...], wave[slot], preferred_element_type=F32).astype(BF)
            near = jnp.concatenate([near[:size], near[size:]], axis=1)
            far = jnp.dot(near, table_b[...], preferred_element_type=F32)
            fr, fi = far[:, :size], far[:, size:]
            scale = lax.rsqrt(jnp.maximum(fr * fr + fi * fi, FLOOR * FLOOR))
            fetch(index).wait()
            factor = 1.0 - levels[index].astype(F32) * scale
            mis[slot, :size, :] = (fr * factor).astype(BF)
            mis[slot, size:, :] = (fi * factor).astype(BF)
        updates = []
        for slot, _ in enumerate(work):
            back = jnp.dot(table_b[...], mis[slot], preferred_element_type=F32).astype(BF)
            back = jnp.concatenate([back[:size], back[size:]], axis=1)
            updates.append(jnp.dot(back, table_a[...], preferred_element_type=F32))
        for slot, (index, top, base, shift) in enumerate(work):
            update = updates[slot]
            fresh = lane >= shift
            for k in range(row_chunks):
                span = slice(k * CHUNK, (k + 1) * CHUNK)
                ur, ui = update[span, :size], update[span, size:]
                pr, pi = probe[0, span, :], probe[1, span, :]
                re, im = patch[slot, 0, span, :], patch[slot, 1, span, :]
                sums[0, span, :] += re * ur + im * ui
                sums[1, span, :] += re * ui - im * ur
                grads = (pr * ur + pi * ui, pr * ui - pi * ur)
                for c in range(2):
                    grad = grads[c].astype(BF).astype(F32)
                    first = pltpu.roll(grad[:, :LANES], shift, 1)
                    second = pltpu.roll(grad[:, LANES:], shift, 1)
                    pieces = (
                        jnp.where(fresh, first, 0.0),
                        jnp.where(fresh, second, first),
                        jnp.where(fresh, 0.0, second),
                    )
                    for j, piece in enumerate(pieces):
                        acc[c, base + j, pl.ds(top + k * CHUNK, CHUNK), :] += piece

    done = 0
    for group in GROUPS:
        times = (count - done) // group

        def several(index, carry, first=done, group=group):
            frames([first + index * group + i for i in range(group)])
            return carry

        lax.fori_loop(0, times, several, 0)
        done = done + times * group
    for j in range(all_tiles):
        inside = j < inner_tiles
        at = (j if inside else j - inner_tiles) * LANES
        upper = own_out if inside else right_out
        upper[:, :, at : at + LANES] = acc[:, j, :rows, :].astype(upper.dtype)
        lower = (low_left if j < left_tiles else low_right) if inside else corner_out
        at = at if j < left_tiles or not inside else at - size
        lower[:, :, at : at + LANES] = acc[:, j, rows:, :].astype(lower.dtype)
    for j in range(N_Y):
        inner = lax.rem(y + j, N_Y) * quarter
        keep_at = pl.multiple_of(core * half + inner, quarter)
        send_at = pl.multiple_of((1 - core) * half + inner, quarter)
        keep_out[j] = sums[:, pl.ds(keep_at, quarter), :]
        send_out[j] = sums[:, pl.ds(send_at, quarter), :]


def run_frames(place, counts, pos, obj, halos, pieces, amps, tables, iteration):
    rows, cols = obj.shape[1], obj.shape[2]
    slots, size = amps.shape[1], amps.shape[2]
    vmem = pl.BlockSpec(memory_space=pltpu.VMEM)
    smem = pl.BlockSpec(memory_space=pltpu.SMEM)
    quarter = size // (N_CORE * N_Y)
    shapes = [
        jax.ShapeDtypeStruct((2, rows, cols), F32),
        jax.ShapeDtypeStruct((2, size, size), F32),
        jax.ShapeDtypeStruct((2, size, cols - size), BF),
        jax.ShapeDtypeStruct((2, rows, size), BF),
        jax.ShapeDtypeStruct((2, size, size), BF),
        jax.ShapeDtypeStruct((N_Y, 3, quarter, size), F32),
        jax.ShapeDtypeStruct((N_Y, 3, quarter, size), F32),
        jax.ShapeDtypeStruct((1, 1), F32),
    ]
    scratch = [
        pltpu.VMEM((2, (cols + size) // LANES, rows + size, LANES), F32),
        pltpu.VMEM((2, (cols + size) // LANES, rows + size, LANES), F32),
        pltpu.VMEM((3, size, size), F32),
        pltpu.VMEM((GROUPS[0], 2 * size, size), BF),
        pltpu.VMEM((GROUPS[0], 2 * size, size), BF),
        pltpu.VMEM((GROUPS[0], 2, size, size), F32),
        pltpu.VMEM((slots, size, size), BF),
        pltpu.SemaphoreType.DMA((slots,)),
    ]
    if len(pieces) > 1:
        scratch.append(pltpu.VMEM((2, size, size), F32))
    return pl.pallas_call(
        functools.partial(frames_kernel, iteration, len(pieces)),
        out_shape=shapes,
        in_specs=[smem] * 3 + [vmem] * (5 + len(pieces)) + [pl.BlockSpec(memory_space=pl.ANY)] + [vmem] * 2,
        out_specs=[vmem] * 7 + [smem],
        scratch_shapes=scratch,
        compiler_params=pltpu.CompilerParams(vmem_limit_bytes=26 << 20),
        cost_estimate=pl.CostEstimate(flops=6_000_000_000, bytes_accessed=8_000_000, transcendentals=0),
        name="frames",
    )(place, counts, pos, obj, *halos, *pieces, amps, *tables)


def update_kernel(with_sum, obj, own, left, low_left, low_right, step, *rest):
    if with_sum:
        totals, (obj_out, halo_left, halo_right, right_out, total_out) = rest[:4], rest[4:]
        total_out[...] = totals[0][...] + totals[1][...] + totals[2][...] + totals[3][...]
    else:
        (obj_out,) = rest
    size = left.shape[2]
    alpha = step[0, 0]
    obj_out[:, :, :size] = obj[:, :, :size] - alpha * (own[:, :, :size] + left[...].astype(F32))
    obj_out[:, size:, size:] = obj[:, size:, size:] - alpha * own[:, size:, size:]
    obj_out[:, :size, :size] -= alpha * low_left[...].astype(F32)
    obj_out[:, :size, size:] = obj[:, :size, size:] - alpha * (own[:, :size, size:] + low_right[...].astype(F32))
    if with_sum:
        halo_left[...] = obj_out[:, :size, :size].astype(BF)
        halo_right[...] = obj_out[:, :size, size:].astype(BF)
        right_out[...] = obj_out[:, :, :size].astype(BF)


def run_update(obj, own, left, low_left, low_right, step, totals):
    rows, cols = obj.shape[1], obj.shape[2]
    size = left.shape[2]
    vmem = pl.BlockSpec(memory_space=pltpu.VMEM)
    smem = pl.BlockSpec(memory_space=pltpu.SMEM)
    shapes = [jax.ShapeDtypeStruct((2, rows, cols), F32)]
    if totals:
        shapes += [
            jax.ShapeDtypeStruct((2, size, size), BF),
            jax.ShapeDtypeStruct((2, size, cols - size), BF),
            jax.ShapeDtypeStruct((2, rows, size), BF),
            jax.ShapeDtypeStruct(totals[0].shape, F32),
        ]
    return pl.pallas_call(
        functools.partial(update_kernel, bool(totals)),
        out_shape=shapes,
        in_specs=[vmem] * 5 + [smem] + [vmem] * len(totals),
        out_specs=[vmem] * len(shapes),
        compiler_params=pltpu.CompilerParams(vmem_limit_bytes=16 << 20),
        cost_estimate=pl.CostEstimate(flops=2_000_000, bytes_accessed=8_000_000, transcendentals=0),
        name="object_update",
    )(obj, own, left, low_left, low_right, step, *totals)


def probe_kernel(place, mine, other, out):
    core, y = place[0], place[1]
    size = out.shape[1]
    half, quarter = size // N_CORE, size // (N_CORE * N_Y)
    for piece, side in ((mine, core), (other, 1 - core)):
        for j in range(N_Y):
            at = pl.multiple_of(side * half + lax.rem(y - j + N_Y, N_Y) * quarter, quarter)
            out[:, pl.ds(at, quarter), :] = piece[j]


def run_probe(place, mine, other):
    vmem = pl.BlockSpec(memory_space=pltpu.VMEM)
    size = mine.shape[-1]
    return pl.pallas_call(
        probe_kernel,
        out_shape=jax.ShapeDtypeStruct((2, size, size), F32),
        in_specs=[pl.BlockSpec(memory_space=pltpu.SMEM), vmem, vmem],
        out_specs=vmem,
        name="probe_whole",
    )(place, mine, other)


def moved(value, axis, count, steps):
    first, last = max(0, -steps), min(count, count - steps)
    return lax.ppermute(value, axis, [(s, s + steps) for s in range(first, last)])


def turned(value, axis, steps):
    return lax.ppermute(value, axis, [(s, (s + steps) % 4) for s in range(4)])


def swapped(value):
    return lax.ppermute(value, "core", [(0, 1), (1, 0)])


def halo(low_left, low_right, right):
    first = moved(low_left, ROW, N_ROW, -1)
    beside = moved(right, COL, N_COL, -1)
    second = moved(low_right, ROW, N_ROW, -1)
    corner = moved(first, COL, N_COL, -1)
    return (first, second, beside, corner)


def rims(low_left, low_right, right, corner):
    corner = moved(corner, COL, N_COL, 1)
    left = moved(right, COL, N_COL, 1)
    second = moved(low_right, ROW, N_ROW, 1)
    first = moved((low_left + corner.astype(F32)).astype(BF), ROW, N_ROW, 1)
    return (left, first, second)


def around(value, axis):
    return [value] + [turned(value, axis, j) for j in (1, 2, 3)]


def column_sum(keep, send):
    part = keep + swapped(send)
    return part[0] + turned(part[1], "y", 1) + turned(part[2], "y", 2) + turned(part[3], "y", 3)


def gathered(mine, total):
    fresh = mine - total[:2] / (total[2] + 1.0)
    half = jnp.stack(around(fresh, "y"))
    return (half, swapped(half))


def local(tables, obj, probe, amps, positions, counts):
    size = probe.shape[-1]
    half, quarter = size // N_CORE, size // (N_CORE * N_Y)
    core, y = lax.axis_index("core"), lax.axis_index("y")
    place = jnp.stack([core, y]).astype(jnp.int32)
    mine = lax.dynamic_slice(probe, (0, core * half + y * quarter, 0), (2, quarter, size))
    low_left, low_right = obj[:, :size, :size].astype(BF), obj[:, :size, size:].astype(BF)
    right = obj[:, :, :size].astype(BF)
    pieces = (probe,)
    for iteration in range(ITERS):
        halos = halo(low_left, low_right, right)
        own, low_left, low_right, right, corner, keep, send, step = run_frames(
            place, counts[iteration, 0], positions[iteration], obj, halos, pieces, amps, tables, iteration
        )
        left, above_left, above_right = rims(low_left, low_right, right, corner)
        totals = around(column_sum(keep, send), "z")
        if iteration < ITERS - 1:
            obj, low_left, low_right, right, total = run_update(
                obj, own, left, above_left, above_right, step, totals
            )
        else:
            (obj,) = run_update(obj, own, left, above_left, above_right, step, [])
            total = sum(totals[1:], totals[0])
        total = sum(around(total, "x")[1:], total)
        pieces = gathered(mine, total)
        mine = pieces[0][0]
    return (obj, run_probe(place, *pieces))


def solution(mesh):
    fine = Mesh(mesh.devices.reshape(N_X, N_Z, N_Y, N_CORE), ("x", "z", "y", "core"))
    placed = (
        P(None, ROW, COL),
        P(),
        P(None, ROW + COL, None, None),
        P(None, None, ROW + COL),
        P(None, COL, ROW),
    )
    blocks = tuple(jnp.asarray(block) for block in chirp_blocks(256))
    return jax.shard_map(
        functools.partial(local, blocks),
        mesh=fine, in_specs=placed, out_specs=(P(None, ROW, COL), P()), check_vma=False,
    )
```

```python
import functools

import jax
import jax.numpy as jnp
import ml_dtypes
import numpy as np
from jax import lax
from jax.experimental import pallas as pl
from jax.experimental.pallas import tpu as pltpu
from jax.sharding import Mesh, PartitionSpec as P

ITERS = 2
FLOOR = 0.3
ALPHA = 0.5
LANES = 128
CHUNK = 32
GROUPS = (4, 2, 1)
N_X, N_Z, N_Y, N_CORE = 4, 4, 4, 2
N_ROW, N_COL = N_X * N_Z, N_Y * N_CORE
ROW, COL = ("x", "z"), ("y", "core")
BF, F32 = jnp.bfloat16, jnp.float32


def chirp_blocks(size):
    offset = np.arange(size, dtype=np.int64)
    units = (offset[:, None] - offset[None, :]) ** 2 % (2 * size)
    phase = np.float32(np.pi) * units.astype(np.float32) / np.float32(size)
    scale = np.float32(1.0 / np.sqrt(size))
    real = (np.cos(phase) * scale).astype(ml_dtypes.bfloat16)
    imag = (np.sin(phase) * scale).astype(ml_dtypes.bfloat16)
    forward = np.block([[real, -imag], [imag, real]])
    return forward, np.ascontiguousarray(forward.T)


def frames_kernel(
    iteration, n_pieces,
    place, counts, pos, obj, below_left, below_right, right, corner, *rest,
):
    pieces, (amps, tab_a, tab_b), rest = rest[:n_pieces], rest[n_pieces : n_pieces + 3], rest[n_pieces + 3 :]
    own_out, low_left, low_right, right_out, corner_out, keep_out, send_out, step_out = rest[:8]
    ext, acc, sums, wave, mis, patch, levels, arrived, here, *rest = rest[8:]
    landing, probe_scratch = rest[: 7 + n_pieces], rest[7 + n_pieces :]
    count = counts[0]
    copies = [
        pltpu.make_async_copy(source, target, here.at[i])
        for i, (source, target) in enumerate(
            zip((obj, below_left, below_right, right, corner, *pieces, tab_a, tab_b), landing)
        )
    ]
    for copy in copies:
        copy.start()
    obj, below_left, below_right, right, corner = landing[:5]
    pieces, (table_a, table_b) = landing[5 : 5 + n_pieces], landing[5 + n_pieces :]

    def fetch(index):
        return pltpu.make_async_copy(amps.at[iteration, index], levels.at[index], arrived.at[index])

    def begin(index, carry):
        fetch(index).start()
        return carry

    lax.fori_loop(0, count, begin, 0)
    rows, cols = obj.shape[1], obj.shape[2]
    size = corner.shape[1]
    row_chunks = size // CHUNK
    inner_tiles, all_tiles, left_tiles = cols // LANES, (cols + size) // LANES, size // LANES
    acc[...] = jnp.zeros_like(acc)
    sums[...] = jnp.zeros_like(sums)
    copies[0].wait()
    for copy in copies[1:5]:
        copy.wait()
    for j in range(all_tiles):
        inside = j < inner_tiles
        at = (j if inside else j - inner_tiles) * LANES
        upper = obj if inside else right
        ext[:, j, :rows, :] = upper[:, :, at : at + LANES].astype(BF).astype(F32)
        lower = (below_left if j < left_tiles else below_right) if inside else corner
        at = at if j < left_tiles or not inside else at - size
        ext[:, j, rows:, :] = lower[:, :, at : at + LANES].astype(F32)
    for copy in copies[5:]:
        copy.wait()
    core, y = place[0], place[1]
    half, quarter = size // N_CORE, size // (N_CORE * N_Y)
    if n_pieces == 1:
        (probe,) = pieces
    else:
        (probe,) = probe_scratch
        for piece, side in ((pieces[0], core), (pieces[1], 1 - core)):
            for j in range(N_Y):
                at = pl.multiple_of(side * half + lax.rem(y - j + N_Y, N_Y) * quarter, quarter)
                probe[:, pl.ds(at, quarter), :] = piece[j]
    peak = jnp.max(probe[0] * probe[0] + probe[1] * probe[1])
    step_out[0, 0] = ALPHA / (peak + 1e-6)
    lane = lax.broadcasted_iota(jnp.int32, (CHUNK, LANES), 1)

    def frames(indices):
        work = []
        for index in indices:
            fetch(index).wait()
        for slot, index in enumerate(indices):
            top, left = pos[0, index], pos[1, index]
            base = left // LANES
            shift = left - base * LANES
            back_shift = lax.rem(LANES - shift, LANES)
            whole = lane < LANES - shift
            for k in range(row_chunks):
                span = slice(k * CHUNK, (k + 1) * CHUNK)
                parts = []
                for c in range(2):
                    tiles = [
                        pltpu.roll(ext[c, base + j, pl.ds(top + k * CHUNK, CHUNK), :], back_shift, 1)
                        for j in range(3)
                    ]
                    cut = jnp.concatenate(
                        [jnp.where(whole, tiles[0], tiles[1]), jnp.where(whole, tiles[1], tiles[2])], axis=1
                    )
                    patch[slot, c, span, :] = cut
                    parts.append(cut)
                re, im = parts
                pr, pi = probe[0, span, :], probe[1, span, :]
                wave[slot, span, :] = (pr * re - pi * im).astype(BF)
                wave[slot, size + k * CHUNK : size + (k + 1) * CHUNK, :] = (pr * im + pi * re).astype(BF)
                sums[2, span, :] += re * re + im * im
            work.append((index, top, base, shift))
        for slot, (index, top, base, shift) in enumerate(work):
            near = jnp.dot(table_a[...], wave[slot], preferred_element_type=F32).astype(BF)
            near = jnp.concatenate([near[:size], near[size:]], axis=1)
            far = jnp.dot(near, table_b[...], preferred_element_type=F32)
            fr, fi = far[:, :size], far[:, size:]
            scale = lax.rsqrt(jnp.maximum(fr * fr + fi * fi, FLOOR * FLOOR))
            factor = 1.0 - levels[index].astype(F32) * scale
            mis[slot, :size, :] = (fr * factor).astype(BF)
            mis[slot, size:, :] = (fi * factor).astype(BF)
        updates = []
        for slot, _ in enumerate(work):
            back = jnp.dot(table_b[...], mis[slot], preferred_element_type=F32).astype(BF)
            back = jnp.concatenate([back[:size], back[size:]], axis=1)
            updates.append(jnp.dot(back, table_a[...], preferred_element_type=F32))
        for slot, (index, top, base, shift) in enumerate(work):
            update = updates[slot]
            fresh = lane >= shift
            for k in range(row_chunks):
                span = slice(k * CHUNK, (k + 1) * CHUNK)
                ur, ui = update[span, :size], update[span, size:]
                pr, pi = probe[0, span, :], probe[1, span, :]
                re, im = patch[slot, 0, span, :], patch[slot, 1, span, :]
                sums[0, span, :] += re * ur + im * ui
                sums[1, span, :] += re * ui - im * ur
                grads = (pr * ur + pi * ui, pr * ui - pi * ur)
                for c in range(2):
                    grad = grads[c].astype(BF).astype(F32)
                    first = pltpu.roll(grad[:, :LANES], shift, 1)
                    second = pltpu.roll(grad[:, LANES:], shift, 1)
                    pieces = (
                        jnp.where(fresh, first, 0.0),
                        jnp.where(fresh, second, first),
                        jnp.where(fresh, 0.0, second),
                    )
                    for j, piece in enumerate(pieces):
                        acc[c, base + j, pl.ds(top + k * CHUNK, CHUNK), :] += piece

    done = 0
    for group in GROUPS:
        times = (count - done) // group

        def several(index, carry, first=done, group=group):
            frames([first + index * group + i for i in range(group)])
            return carry

        lax.fori_loop(0, times, several, 0)
        done = done + times * group
    for j in range(all_tiles):
        inside = j < inner_tiles
        at = (j if inside else j - inner_tiles) * LANES
        upper = own_out if inside else right_out
        upper[:, :, at : at + LANES] = acc[:, j, :rows, :].astype(upper.dtype)
        lower = (low_left if j < left_tiles else low_right) if inside else corner_out
        at = at if j < left_tiles or not inside else at - size
        lower[:, :, at : at + LANES] = acc[:, j, rows:, :].astype(lower.dtype)
    for j in range(N_Y):
        inner = lax.rem(y + j, N_Y) * quarter
        keep_at = pl.multiple_of(core * half + inner, quarter)
        send_at = pl.multiple_of((1 - core) * half + inner, quarter)
        keep_out[j] = sums[:, pl.ds(keep_at, quarter), :]
        send_out[j] = sums[:, pl.ds(send_at, quarter), :]


def run_frames(place, counts, pos, obj, halos, pieces, amps, tables, iteration):
    rows, cols = obj.shape[1], obj.shape[2]
    slots, size = amps.shape[1], amps.shape[2]
    vmem = pl.BlockSpec(memory_space=pltpu.VMEM)
    smem = pl.BlockSpec(memory_space=pltpu.SMEM)
    quarter = size // (N_CORE * N_Y)
    shapes = [
        jax.ShapeDtypeStruct((2, rows, cols), F32),
        jax.ShapeDtypeStruct((2, size, size), F32),
        jax.ShapeDtypeStruct((2, size, cols - size), BF),
        jax.ShapeDtypeStruct((2, rows, size), BF),
        jax.ShapeDtypeStruct((2, size, size), BF),
        jax.ShapeDtypeStruct((N_Y, 3, quarter, size), F32),
        jax.ShapeDtypeStruct((N_Y, 3, quarter, size), F32),
        jax.ShapeDtypeStruct((1, 1), F32),
    ]
    scratch = [
        pltpu.VMEM((2, (cols + size) // LANES, rows + size, LANES), F32),
        pltpu.VMEM((2, (cols + size) // LANES, rows + size, LANES), F32),
        pltpu.VMEM((3, size, size), F32),
        pltpu.VMEM((GROUPS[0], 2 * size, size), BF),
        pltpu.VMEM((GROUPS[0], 2 * size, size), BF),
        pltpu.VMEM((GROUPS[0], 2, size, size), F32),
        pltpu.VMEM((slots, size, size), BF),
        pltpu.SemaphoreType.DMA((slots,)),
    ]
    loaded = (obj, *halos, *pieces, *tables)
    scratch.append(pltpu.SemaphoreType.DMA((len(loaded),)))
    scratch += [pltpu.VMEM(value.shape, value.dtype) for value in loaded]
    if len(pieces) > 1:
        scratch.append(pltpu.VMEM((2, size, size), F32))
    return pl.pallas_call(
        functools.partial(frames_kernel, iteration, len(pieces)),
        out_shape=shapes,
        in_specs=[smem] * 3 + [pl.BlockSpec(memory_space=pltpu.HBM)] * (8 + len(pieces)),
        out_specs=[vmem] * 7 + [smem],
        scratch_shapes=scratch,
        compiler_params=pltpu.CompilerParams(vmem_limit_bytes=48 << 20),
        cost_estimate=pl.CostEstimate(flops=6_000_000_000, bytes_accessed=8_000_000, transcendentals=0),
        name="frames",
    )(place, counts, pos, obj, *halos, *pieces, amps, *tables)


def update_kernel(with_sum, obj, own, left, low_left, low_right, step, *rest):
    if with_sum:
        totals, (obj_out, halo_left, halo_right, right_out, total_out) = rest[:4], rest[4:]
        total_out[...] = totals[0][...] + totals[1][...] + totals[2][...] + totals[3][...]
    else:
        (obj_out,) = rest
    size = left.shape[2]
    alpha = step[0, 0]
    obj_out[:, :, :size] = obj[:, :, :size] - alpha * (own[:, :, :size] + left[...].astype(F32))
    obj_out[:, size:, size:] = obj[:, size:, size:] - alpha * own[:, size:, size:]
    obj_out[:, :size, :size] -= alpha * low_left[...].astype(F32)
    obj_out[:, :size, size:] = obj[:, :size, size:] - alpha * (own[:, :size, size:] + low_right[...].astype(F32))
    if with_sum:
        halo_left[...] = obj_out[:, :size, :size].astype(BF)
        halo_right[...] = obj_out[:, :size, size:].astype(BF)
        right_out[...] = obj_out[:, :, :size].astype(BF)


def run_update(obj, own, left, low_left, low_right, step, totals):
    rows, cols = obj.shape[1], obj.shape[2]
    size = left.shape[2]
    vmem = pl.BlockSpec(memory_space=pltpu.VMEM)
    smem = pl.BlockSpec(memory_space=pltpu.SMEM)
    shapes = [jax.ShapeDtypeStruct((2, rows, cols), F32)]
    if totals:
        shapes += [
            jax.ShapeDtypeStruct((2, size, size), BF),
            jax.ShapeDtypeStruct((2, size, cols - size), BF),
            jax.ShapeDtypeStruct((2, rows, size), BF),
            jax.ShapeDtypeStruct(totals[0].shape, F32),
        ]
    return pl.pallas_call(
        functools.partial(update_kernel, bool(totals)),
        out_shape=shapes,
        in_specs=[vmem] * 5 + [smem] + [vmem] * len(totals),
        out_specs=[vmem] * len(shapes),
        compiler_params=pltpu.CompilerParams(vmem_limit_bytes=16 << 20),
        cost_estimate=pl.CostEstimate(flops=2_000_000, bytes_accessed=8_000_000, transcendentals=0),
        name="object_update",
    )(obj, own, left, low_left, low_right, step, *totals)


def probe_kernel(place, mine, other, out):
    core, y = place[0], place[1]
    size = out.shape[1]
    half, quarter = size // N_CORE, size // (N_CORE * N_Y)
    for piece, side in ((mine, core), (other, 1 - core)):
        for j in range(N_Y):
            at = pl.multiple_of(side * half + lax.rem(y - j + N_Y, N_Y) * quarter, quarter)
            out[:, pl.ds(at, quarter), :] = piece[j]


def run_probe(place, mine, other):
    vmem = pl.BlockSpec(memory_space=pltpu.VMEM)
    size = mine.shape[-1]
    return pl.pallas_call(
        probe_kernel,
        out_shape=jax.ShapeDtypeStruct((2, size, size), F32),
        in_specs=[pl.BlockSpec(memory_space=pltpu.SMEM), vmem, vmem],
        out_specs=vmem,
        name="probe_whole",
    )(place, mine, other)


def moved(value, axis, count, steps):
    first, last = max(0, -steps), min(count, count - steps)
    return lax.ppermute(value, axis, [(s, s + steps) for s in range(first, last)])


def turned(value, axis, steps):
    return lax.ppermute(value, axis, [(s, (s + steps) % 4) for s in range(4)])


def swapped(value):
    return lax.ppermute(value, "core", [(0, 1), (1, 0)])


def halo(low_left, low_right, right):
    first = moved(low_left, ROW, N_ROW, -1)
    beside = moved(right, COL, N_COL, -1)
    second = moved(low_right, ROW, N_ROW, -1)
    corner = moved(first, COL, N_COL, -1)
    return (first, second, beside, corner)


def rims(low_left, low_right, right, corner):
    corner = moved(corner, COL, N_COL, 1)
    left = moved(right, COL, N_COL, 1)
    second = moved(low_right, ROW, N_ROW, 1)
    first = moved((low_left + corner.astype(F32)).astype(BF), ROW, N_ROW, 1)
    return (left, first, second)


def around(value, axis):
    return [value] + [turned(value, axis, j) for j in (1, 2, 3)]


def column_sum(keep, send):
    part = keep + swapped(send)
    return part[0] + turned(part[1], "y", 1) + turned(part[2], "y", 2) + turned(part[3], "y", 3)


def gathered(mine, total):
    fresh = mine - total[:2] / (total[2] + 1.0)
    half = jnp.stack(around(fresh, "y"))
    return (half, swapped(half))


def local(tables, obj, probe, amps, positions, counts):
    size = probe.shape[-1]
    half, quarter = size // N_CORE, size // (N_CORE * N_Y)
    core, y = lax.axis_index("core"), lax.axis_index("y")
    place = jnp.stack([core, y]).astype(jnp.int32)
    mine = lax.dynamic_slice(probe, (0, core * half + y * quarter, 0), (2, quarter, size))
    low_left, low_right = obj[:, :size, :size].astype(BF), obj[:, :size, size:].astype(BF)
    right = obj[:, :, :size].astype(BF)
    pieces = (probe,)
    for iteration in range(ITERS):
        halos = halo(low_left, low_right, right)
        own, low_left, low_right, right, corner, keep, send, step = run_frames(
            place, counts[iteration, 0], positions[iteration], obj, halos, pieces, amps, tables, iteration
        )
        left, above_left, above_right = rims(low_left, low_right, right, corner)
        totals = around(column_sum(keep, send), "z")
        if iteration < ITERS - 1:
            obj, low_left, low_right, right, total = run_update(
                obj, own, left, above_left, above_right, step, totals
            )
        else:
            (obj,) = run_update(obj, own, left, above_left, above_right, step, [])
            total = sum(totals[1:], totals[0])
        total = sum(around(total, "x")[1:], total)
        pieces = gathered(mine, total)
        mine = pieces[0][0]
    return (obj, run_probe(place, *pieces))


def solution(mesh):
    fine = Mesh(mesh.devices.reshape(N_X, N_Z, N_Y, N_CORE), ("x", "z", "y", "core"))
    placed = (
        P(None, ROW, COL),
        P(),
        P(None, ROW + COL, None, None),
        P(None, None, ROW + COL),
        P(None, COL, ROW),
    )
    blocks = tuple(jnp.asarray(block) for block in chirp_blocks(256))
    return jax.shard_map(
        functools.partial(local, blocks),
        mesh=fine, in_specs=placed, out_specs=(P(None, ROW, COL), P()), check_vma=False,
    )
```

```python
import functools

import jax
import jax.numpy as jnp
import ml_dtypes
import numpy as np
from jax import lax
from jax.experimental import pallas as pl
from jax.experimental.pallas import tpu as pltpu
from jax.sharding import Mesh, PartitionSpec as P

ITERS = 2
FLOOR = 0.3
ALPHA = 0.5
LANES = 128
CHUNK = 32
GROUPS = (4, 2, 1)
N_X, N_Z, N_Y, N_CORE = 4, 4, 4, 2
N_ROW, N_COL = N_X * N_Z, N_Y * N_CORE
ROW, COL = ("x", "z"), ("y", "core")
BF, F32 = jnp.bfloat16, jnp.float32


def chirp_blocks(size):
    offset = np.arange(size, dtype=np.int64)
    units = (offset[:, None] - offset[None, :]) ** 2 % (2 * size)
    phase = np.float32(np.pi) * units.astype(np.float32) / np.float32(size)
    scale = np.float32(1.0 / np.sqrt(size))
    real = (np.cos(phase) * scale).astype(ml_dtypes.bfloat16)
    imag = (np.sin(phase) * scale).astype(ml_dtypes.bfloat16)
    forward = np.block([[real, -imag], [imag, real]])
    return forward, np.ascontiguousarray(forward.T)


def frames_kernel(
    iteration, n_pieces,
    place, counts, pos, obj, below, right, corner, *rest,
):
    pieces, (amps, tab_a, tab_b), rest = rest[:n_pieces], rest[n_pieces : n_pieces + 3], rest[n_pieces + 3 :]
    own_out, low_left, low_right, right_out, corner_out, keep_out, send_out, step_out = rest[:8]
    ext, acc, sums, wave, mis, patch, levels, arrived, here, *rest = rest[8:]
    landing, probe_scratch = rest[: 6 + n_pieces], rest[6 + n_pieces :]
    count = counts[0]
    copies = [
        pltpu.make_async_copy(source, target, here.at[i])
        for i, (source, target) in enumerate(
            zip((obj, below, right, corner, *pieces, tab_a, tab_b), landing)
        )
    ]
    for copy in copies:
        copy.start()
    obj, below, right, corner = landing[:4]
    pieces, (table_a, table_b) = landing[4 : 4 + n_pieces], landing[4 + n_pieces :]

    def fetch(index):
        return pltpu.make_async_copy(amps.at[iteration, index], levels.at[index], arrived.at[index])

    def begin(index, carry):
        fetch(index).start()
        return carry

    lax.fori_loop(0, count, begin, 0)
    rows, cols = obj.shape[1], obj.shape[2]
    size = corner.shape[1]
    row_chunks = size // CHUNK
    inner_tiles, all_tiles, left_tiles = cols // LANES, (cols + size) // LANES, size // LANES
    acc[...] = jnp.zeros_like(acc)
    sums[...] = jnp.zeros_like(sums)
    copies[0].wait()
    for copy in copies[1:4]:
        copy.wait()
    for j in range(all_tiles):
        inside = j < inner_tiles
        at = (j if inside else j - inner_tiles) * LANES
        upper = obj if inside else right
        ext[:, j, :rows, :] = upper[:, :, at : at + LANES].astype(BF).astype(F32)
        lower = below if inside else corner
        ext[:, j, rows:, :] = lower[:, :, at : at + LANES].astype(F32)
    for copy in copies[4:]:
        copy.wait()
    core, y = place[0], place[1]
    half, quarter = size // N_CORE, size // (N_CORE * N_Y)
    if n_pieces == 1:
        (probe,) = pieces
    else:
        (probe,) = probe_scratch
        for piece, side in ((pieces[0], core), (pieces[1], 1 - core)):
            for j in range(N_Y):
                at = pl.multiple_of(side * half + lax.rem(y - j + N_Y, N_Y) * quarter, quarter)
                probe[:, pl.ds(at, quarter), :] = piece[j]
    peak = jnp.max(probe[0] * probe[0] + probe[1] * probe[1])
    step_out[0, 0] = ALPHA / (peak + 1e-6)
    lane = lax.broadcasted_iota(jnp.int32, (CHUNK, LANES), 1)

    def frames(indices):
        work = []
        for index in indices:
            fetch(index).wait()
        for slot, index in enumerate(indices):
            top, left = pos[0, index], pos[1, index]
            base = left // LANES
            shift = left - base * LANES
            back_shift = lax.rem(LANES - shift, LANES)
            whole = lane < LANES - shift
            for k in range(row_chunks):
                span = slice(k * CHUNK, (k + 1) * CHUNK)
                parts = []
                for c in range(2):
                    tiles = [
                        pltpu.roll(ext[c, base + j, pl.ds(top + k * CHUNK, CHUNK), :], back_shift, 1)
                        for j in range(3)
                    ]
                    cut = jnp.concatenate(
                        [jnp.where(whole, tiles[0], tiles[1]), jnp.where(whole, tiles[1], tiles[2])], axis=1
                    )
                    patch[slot, c, span, :] = cut
                    parts.append(cut)
                re, im = parts
                pr, pi = probe[0, span, :], probe[1, span, :]
                wave[slot, span, :] = (pr * re - pi * im).astype(BF)
                wave[slot, size + k * CHUNK : size + (k + 1) * CHUNK, :] = (pr * im + pi * re).astype(BF)
                sums[2, span, :] += re * re + im * im
            work.append((index, top, base, shift))
        for slot, (index, top, base, shift) in enumerate(work):
            near = jnp.dot(table_a[...], wave[slot], preferred_element_type=F32).astype(BF)
            near = jnp.concatenate([near[:size], near[size:]], axis=1)
            far = jnp.dot(near, table_b[...], preferred_element_type=F32)
            fr, fi = far[:, :size], far[:, size:]
            scale = lax.rsqrt(jnp.maximum(fr * fr + fi * fi, FLOOR * FLOOR))
            factor = 1.0 - levels[index].astype(F32) * scale
            mis[slot, :size, :] = (fr * factor).astype(BF)
            mis[slot, size:, :] = (fi * factor).astype(BF)
        updates = []
        for slot, _ in enumerate(work):
            back = jnp.dot(table_b[...], mis[slot], preferred_element_type=F32).astype(BF)
            back = jnp.concatenate([back[:size], back[size:]], axis=1)
            updates.append(jnp.dot(back, table_a[...], preferred_element_type=F32))
        for slot, (index, top, base, shift) in enumerate(work):
            update = updates[slot]
            fresh = lane >= shift
            for k in range(row_chunks):
                span = slice(k * CHUNK, (k + 1) * CHUNK)
                ur, ui = update[span, :size], update[span, size:]
                pr, pi = probe[0, span, :], probe[1, span, :]
                re, im = patch[slot, 0, span, :], patch[slot, 1, span, :]
                sums[0, span, :] += re * ur + im * ui
                sums[1, span, :] += re * ui - im * ur
                grads = (pr * ur + pi * ui, pr * ui - pi * ur)
                for c in range(2):
                    grad = grads[c].astype(BF).astype(F32)
                    first = pltpu.roll(grad[:, :LANES], shift, 1)
                    second = pltpu.roll(grad[:, LANES:], shift, 1)
                    pieces = (
                        jnp.where(fresh, first, 0.0),
                        jnp.where(fresh, second, first),
                        jnp.where(fresh, 0.0, second),
                    )
                    for j, piece in enumerate(pieces):
                        acc[c, base + j, pl.ds(top + k * CHUNK, CHUNK), :] += piece

    done = 0
    for group in GROUPS:
        times = (count - done) // group

        def several(index, carry, first=done, group=group):
            frames([first + index * group + i for i in range(group)])
            return carry

        lax.fori_loop(0, times, several, 0)
        done = done + times * group
    for j in range(all_tiles):
        inside = j < inner_tiles
        at = (j if inside else j - inner_tiles) * LANES
        upper = own_out if inside else right_out
        upper[:, :, at : at + LANES] = acc[:, j, :rows, :].astype(upper.dtype)
        lower = (low_left if j < left_tiles else low_right) if inside else corner_out
        at = at if j < left_tiles or not inside else at - size
        lower[:, :, at : at + LANES] = acc[:, j, rows:, :].astype(lower.dtype)
    for j in range(N_Y):
        inner = lax.rem(y + j, N_Y) * quarter
        keep_at = pl.multiple_of(core * half + inner, quarter)
        send_at = pl.multiple_of((1 - core) * half + inner, quarter)
        keep_out[j] = sums[:, pl.ds(keep_at, quarter), :]
        send_out[j] = sums[:, pl.ds(send_at, quarter), :]


def run_frames(place, counts, pos, obj, halos, pieces, amps, tables, iteration):
    rows, cols = obj.shape[1], obj.shape[2]
    slots, size = amps.shape[1], amps.shape[2]
    vmem = pl.BlockSpec(memory_space=pltpu.VMEM)
    smem = pl.BlockSpec(memory_space=pltpu.SMEM)
    quarter = size // (N_CORE * N_Y)
    shapes = [
        jax.ShapeDtypeStruct((2, rows, cols), F32),
        jax.ShapeDtypeStruct((2, size, size), F32),
        jax.ShapeDtypeStruct((2, size, cols - size), BF),
        jax.ShapeDtypeStruct((2, rows, size), BF),
        jax.ShapeDtypeStruct((2, size, size), BF),
        jax.ShapeDtypeStruct((N_Y, 3, quarter, size), F32),
        jax.ShapeDtypeStruct((N_Y, 3, quarter, size), F32),
        jax.ShapeDtypeStruct((1, 1), F32),
    ]
    scratch = [
        pltpu.VMEM((2, (cols + size) // LANES, rows + size, LANES), F32),
        pltpu.VMEM((2, (cols + size) // LANES, rows + size, LANES), F32),
        pltpu.VMEM((3, size, size), F32),
        pltpu.VMEM((GROUPS[0], 2 * size, size), BF),
        pltpu.VMEM((GROUPS[0], 2 * size, size), BF),
        pltpu.VMEM((GROUPS[0], 2, size, size), F32),
        pltpu.VMEM((slots, size, size), BF),
        pltpu.SemaphoreType.DMA((slots,)),
    ]
    loaded = (obj, *halos, *pieces, *tables)
    scratch.append(pltpu.SemaphoreType.DMA((len(loaded),)))
    scratch += [pltpu.VMEM(value.shape, value.dtype) for value in loaded]
    if len(pieces) > 1:
        scratch.append(pltpu.VMEM((2, size, size), F32))
    return pl.pallas_call(
        functools.partial(frames_kernel, iteration, len(pieces)),
        out_shape=shapes,
        in_specs=[smem] * 3 + [pl.BlockSpec(memory_space=pltpu.HBM)] * (7 + len(pieces)),
        out_specs=[vmem] * 7 + [smem],
        scratch_shapes=scratch,
        compiler_params=pltpu.CompilerParams(vmem_limit_bytes=48 << 20),
        cost_estimate=pl.CostEstimate(flops=6_000_000_000, bytes_accessed=8_000_000, transcendentals=0),
        name="frames",
    )(place, counts, pos, obj, *halos, *pieces, amps, *tables)


def spec(space):
    return pl.BlockSpec(memory_space=space)


def small_call(body, shapes, operands, name, limit=16):
    spaces = [pltpu.SMEM if v.size <= 2 else pltpu.VMEM for v in operands[0]] + [pl.ANY] * len(operands[1])
    return pl.pallas_call(
        body,
        out_shape=shapes,
        in_specs=[spec(space) for space in spaces],
        out_specs=[spec(pltpu.VMEM)] * len(shapes),
        compiler_params=pltpu.CompilerParams(vmem_limit_bytes=limit << 20),
        cost_estimate=pl.CostEstimate(flops=2_000_000, bytes_accessed=4_000_000, transcendentals=0),
        name=name,
    )(*operands[0], *operands[1])


def y_kernel(a, b, c, d, low_left, low_right, corner, total, down):
    size = low_left.shape[2]
    total[...] = a[0] + b[...] + c[...] + d[...]
    down[:, :, :size] = (low_left[...] + corner[...].astype(F32)).astype(BF)
    down[:, :, size:] = low_right[...]


def z_kernel(a, b, c, d, waited, total):
    total[...] = a[...] + b[...] + c[...] + d[...]


def probe_step(a, b, c, d, mine, fresh):
    total = a[...] + b[...] + c[...] + d[...]
    fresh[...] = mine[...] - total[:2] / (total[2:] + 1.0)


def x_kernel(a, b, c, d, mine, waited, fresh):
    probe_step(a, b, c, d, mine, fresh)


def object_step(obj, own, left, down, step, obj_out):
    size = left.shape[2]
    alpha = step[0, 0]
    obj_out[:, :, :size] = obj[:, :, :size] - alpha * (own[:, :, :size] + left[...].astype(F32))
    obj_out[:, :size, :size] -= alpha * down[:, :, :size].astype(F32)
    obj_out[:, :size, size:] = obj[:, :size, size:] - alpha * (own[:, :size, size:] + down[:, :, size:].astype(F32))
    obj_out[:, size:, size:] = obj[:, size:, size:] - alpha * own[:, size:, size:]


def both_kernel(a, b, c, d, mine, obj, own, left, down, step, fresh, obj_out, below, right):
    probe_step(a, b, c, d, mine, fresh)
    object_step(obj, own, left, down, step, obj_out)
    size = left.shape[2]
    below[...] = obj_out[:, :size, :].astype(BF)
    right[...] = obj_out[:, :, :size].astype(BF)


def probe_kernel(place, mine, other, out):
    core, y = place[0], place[1]
    size = out.shape[1]
    half, quarter = size // N_CORE, size // (N_CORE * N_Y)
    for piece, side in ((mine, core), (other, 1 - core)):
        for j in range(N_Y):
            at = pl.multiple_of(side * half + lax.rem(y - j + N_Y, N_Y) * quarter, quarter)
            out[:, pl.ds(at, quarter), :] = piece[j]


def run_probe(place, mine, other):
    vmem = pl.BlockSpec(memory_space=pltpu.VMEM)
    size = mine.shape[-1]
    return pl.pallas_call(
        probe_kernel,
        out_shape=jax.ShapeDtypeStruct((2, size, size), F32),
        in_specs=[pl.BlockSpec(memory_space=pltpu.SMEM), vmem, vmem],
        out_specs=vmem,
        name="probe_whole",
    )(place, mine, other)


def moved(value, axis, count, steps):
    first, last = max(0, -steps), min(count, count - steps)
    return lax.ppermute(value, axis, [(s, s + steps) for s in range(first, last)])


def turned(value, axis, steps):
    return lax.ppermute(value, axis, [(s, (s + steps) % 4) for s in range(4)])


def swapped(value):
    return lax.ppermute(value, "core", [(0, 1), (1, 0)])


def halo(below, right):
    size = below.shape[1]
    below = moved(below, ROW, N_ROW, -1)
    right = moved(right, COL, N_COL, -1)
    corner = moved(below[:, :, :size], COL, N_COL, -1)
    return (below, right, corner)


def around(value, axis):
    return [value] + [turned(value, axis, j) for j in (1, 2, 3)]


def local(tables, obj, probe, amps, positions, counts):
    rows, cols = obj.shape[1], obj.shape[2]
    size = probe.shape[-1]
    half, quarter = size // N_CORE, size // (N_CORE * N_Y)
    core, y = lax.axis_index("core"), lax.axis_index("y")
    place = jnp.stack([core, y]).astype(jnp.int32)
    mine = lax.dynamic_slice(probe, (0, core * half + y * quarter, 0), (2, quarter, size))
    whole = jax.ShapeDtypeStruct(obj.shape, F32)
    flat = jax.ShapeDtypeStruct((2, size, cols), BF)
    tall = jax.ShapeDtypeStruct((2, rows, size), BF)
    share = jax.ShapeDtypeStruct((3, quarter, size), F32)
    part = jax.ShapeDtypeStruct(mine.shape, F32)
    below, right = obj[:, :size, :].astype(BF), obj[:, :, :size].astype(BF)
    pieces = (probe,)
    for iteration in range(ITERS):
        halos = halo(below, right)
        own, low_left, low_right, right, corner, keep, send, step = run_frames(
            place, counts[iteration, 0], positions[iteration], obj, halos, pieces, amps, tables, iteration
        )
        corner = moved(corner, COL, N_COL, 1)
        left = moved(right, COL, N_COL, 1)
        sums = keep + swapped(send)
        sums = [sums[:1]] + [turned(sums[j], "y", j) for j in (1, 2, 3)]
        total, down = small_call(y_kernel, [share, flat], ([*sums, low_left, low_right, corner], []), "y_sum")
        down = moved(down, ROW, N_ROW, 1)
        (total,) = small_call(z_kernel, [share], (around(total, "z"), [left]), "z_sum")
        sums = around(total, "x") + [mine]
        if iteration < ITERS - 1:
            mine, obj, below, right = small_call(
                both_kernel, [part, whole, flat, tall], ([*sums, obj, own, left, down, step], []), "x_sum_object"
            )
        else:
            (mine,) = small_call(x_kernel, [part], (sums, [down]), "x_sum")
            (obj,) = small_call(object_step, [whole], ([obj, own, left, down, step], []), "object_update")
        stack = jnp.stack(around(mine, "y"))
        pieces = (stack, swapped(stack))
    return (obj, run_probe(place, *pieces))


def solution(mesh):
    fine = Mesh(mesh.devices.reshape(N_X, N_Z, N_Y, N_CORE), ("x", "z", "y", "core"))
    placed = (
        P(None, ROW, COL),
        P(),
        P(None, ROW + COL, None, None),
        P(None, None, ROW + COL),
        P(None, COL, ROW),
    )
    blocks = tuple(jnp.asarray(block) for block in chirp_blocks(256))
    return jax.shard_map(
        functools.partial(local, blocks),
        mesh=fine, in_specs=placed, out_specs=(P(None, ROW, COL), P()), check_vma=False,
    )
```

```python
import functools

import jax
import jax.numpy as jnp
import ml_dtypes
import numpy as np
from jax import lax
from jax.experimental import pallas as pl
from jax.experimental.pallas import tpu as pltpu
from jax.sharding import Mesh, PartitionSpec as P

ITERS = 2
FLOOR = 0.3
ALPHA = 0.5
LANES = 128
CHUNK = 32
GROUPS = (4, 2, 1)
N_X, N_Z, N_Y, N_CORE = 4, 4, 4, 2
N_ROW, N_COL = N_X * N_Z, N_Y * N_CORE
ROW, COL = ("x", "z"), ("y", "core")
BF, F32 = jnp.bfloat16, jnp.float32


def chirp_blocks(size):
    offset = np.arange(size, dtype=np.int64)
    units = (offset[:, None] - offset[None, :]) ** 2 % (2 * size)
    phase = np.float32(np.pi) * units.astype(np.float32) / np.float32(size)
    scale = np.float32(1.0 / np.sqrt(size))
    real = (np.cos(phase) * scale).astype(ml_dtypes.bfloat16)
    imag = (np.sin(phase) * scale).astype(ml_dtypes.bfloat16)
    forward = np.block([[real, -imag], [imag, real]])
    return np.stack([forward, forward.T])


def frames_kernel(
    iteration, n_low, n_pieces,
    place, counts, pos, obj, *rest,
):
    lows, (right, corner), rest = rest[:n_low], rest[n_low : n_low + 2], rest[n_low + 2 :]
    pieces, (amps, tables), rest = rest[:n_pieces], rest[n_pieces : n_pieces + 2], rest[n_pieces + 2 :]
    own_out, low_left, low_right, right_out, corner_out, keep_out, send_out, step_out = rest[:8]
    ext, acc, sums, wave, mis, patch, levels, arrived, here, *rest = rest[8:]
    landing, probe_scratch = rest[: 5 + n_pieces], rest[5 + n_pieces :]
    count = counts[0]
    low_parts, at = [], 0
    for low in lows:
        low_parts.append(landing[1].at[:, :, at : at + low.shape[2]])
        at += low.shape[2]
    sources = (obj, right, corner, *lows, *pieces, tables)
    targets = (landing[0], *landing[2:4], *low_parts, *landing[4:])
    copies = [
        pltpu.make_async_copy(source, target, here.at[i])
        for i, (source, target) in enumerate(zip(sources, targets))
    ]
    for copy in copies:
        copy.start()
    obj, below, right, corner = landing[:4]
    pieces, tables = landing[4 : 4 + n_pieces], landing[4 + n_pieces]
    table_a, table_b = tables.at[0], tables.at[1]

    def fetch(index):
        return pltpu.make_async_copy(amps.at[iteration, index], levels.at[index], arrived.at[index])

    def begin(index, carry):
        fetch(index).start()
        return carry

    lax.fori_loop(0, count, begin, 0)
    rows, cols = obj.shape[1], obj.shape[2]
    size = corner.shape[1]
    row_chunks = size // CHUNK
    inner_tiles, all_tiles, left_tiles = cols // LANES, (cols + size) // LANES, size // LANES
    acc[...] = jnp.zeros_like(acc)
    sums[...] = jnp.zeros_like(sums)
    copies[0].wait()
    for copy in copies[1 : 3 + n_low]:
        copy.wait()
    for j in range(all_tiles):
        inside = j < inner_tiles
        at = (j if inside else j - inner_tiles) * LANES
        upper = obj if inside else right
        ext[:, j, :rows, :] = upper[:, :, at : at + LANES].astype(BF).astype(F32)
        lower = below if inside else corner
        ext[:, j, rows:, :] = lower[:, :, at : at + LANES].astype(F32)
    for copy in copies[3 + n_low :]:
        copy.wait()
    core, x = place[0], place[1]
    half, quarter = size // N_CORE, size // (N_CORE * N_X)
    if n_pieces == 1:
        (probe,) = pieces
    else:
        (probe,) = probe_scratch
        for piece, side in ((pieces[0], core), (pieces[1], 1 - core)):
            for j in range(N_X):
                at = pl.multiple_of(side * half + lax.rem(x - j + N_X, N_X) * quarter, quarter)
                probe[:, pl.ds(at, quarter), :] = piece[j]
    peak = jnp.max(probe[0] * probe[0] + probe[1] * probe[1])
    step_out[0, 0] = ALPHA / (peak + 1e-6)
    lane = lax.broadcasted_iota(jnp.int32, (CHUNK, LANES), 1)

    def frames(indices):
        work = []
        for index in indices:
            fetch(index).wait()
        for slot, index in enumerate(indices):
            top, left = pos[0, index], pos[1, index]
            base = left // LANES
            shift = left - base * LANES
            back_shift = lax.rem(LANES - shift, LANES)
            whole = lane < LANES - shift
            for k in range(row_chunks):
                span = slice(k * CHUNK, (k + 1) * CHUNK)
                parts = []
                for c in range(2):
                    tiles = [
                        pltpu.roll(ext[c, base + j, pl.ds(top + k * CHUNK, CHUNK), :], back_shift, 1)
                        for j in range(3)
                    ]
                    cut = jnp.concatenate(
                        [jnp.where(whole, tiles[0], tiles[1]), jnp.where(whole, tiles[1], tiles[2])], axis=1
                    )
                    patch[slot, c, span, :] = cut
                    parts.append(cut)
                re, im = parts
                pr, pi = probe[0, span, :], probe[1, span, :]
                wave[slot, span, :] = (pr * re - pi * im).astype(BF)
                wave[slot, size + k * CHUNK : size + (k + 1) * CHUNK, :] = (pr * im + pi * re).astype(BF)
                sums[2, span, :] += re * re + im * im
            work.append((index, top, base, shift))
        for slot, (index, top, base, shift) in enumerate(work):
            near = jnp.dot(table_a[...], wave[slot], preferred_element_type=F32).astype(BF)
            near = jnp.concatenate([near[:size], near[size:]], axis=1)
            far = jnp.dot(near, table_b[...], preferred_element_type=F32)
            fr, fi = far[:, :size], far[:, size:]
            scale = lax.rsqrt(jnp.maximum(fr * fr + fi * fi, FLOOR * FLOOR))
            factor = 1.0 - levels[index].astype(F32) * scale
            mis[slot, :size, :] = (fr * factor).astype(BF)
            mis[slot, size:, :] = (fi * factor).astype(BF)
        updates = []
        for slot, _ in enumerate(work):
            back = jnp.dot(table_b[...], mis[slot], preferred_element_type=F32).astype(BF)
            back = jnp.concatenate([back[:size], back[size:]], axis=1)
            updates.append(jnp.dot(back, table_a[...], preferred_element_type=F32))
        for slot, (index, top, base, shift) in enumerate(work):
            update = updates[slot]
            fresh = lane >= shift
            for k in range(row_chunks):
                span = slice(k * CHUNK, (k + 1) * CHUNK)
                ur, ui = update[span, :size], update[span, size:]
                pr, pi = probe[0, span, :], probe[1, span, :]
                re, im = patch[slot, 0, span, :], patch[slot, 1, span, :]
                sums[0, span, :] += re * ur + im * ui
                sums[1, span, :] += re * ui - im * ur
                grads = (pr * ur + pi * ui, pr * ui - pi * ur)
                for c in range(2):
                    grad = grads[c].astype(BF).astype(F32)
                    first = pltpu.roll(grad[:, :LANES], shift, 1)
                    second = pltpu.roll(grad[:, LANES:], shift, 1)
                    pieces = (
                        jnp.where(fresh, first, 0.0),
                        jnp.where(fresh, second, first),
                        jnp.where(fresh, 0.0, second),
                    )
                    for j, piece in enumerate(pieces):
                        acc[c, base + j, pl.ds(top + k * CHUNK, CHUNK), :] += piece

    done = 0
    for group in GROUPS:
        times = (count - done) // group

        def several(index, carry, first=done, group=group):
            frames([first + index * group + i for i in range(group)])
            return carry

        lax.fori_loop(0, times, several, 0)
        done = done + times * group
    for j in range(all_tiles):
        inside = j < inner_tiles
        at = (j if inside else j - inner_tiles) * LANES
        upper = own_out if inside else right_out
        upper[:, :, at : at + LANES] = acc[:, j, :rows, :].astype(upper.dtype)
        lower = (low_left if j < left_tiles else low_right) if inside else corner_out
        at = at if j < left_tiles or not inside else at - size
        lower[:, :, at : at + LANES] = acc[:, j, rows:, :].astype(lower.dtype)
    for j in range(N_X):
        inner = lax.rem(x + j, N_X) * quarter
        keep_at = pl.multiple_of(core * half + inner, quarter)
        send_at = pl.multiple_of((1 - core) * half + inner, quarter)
        keep_out[j] = sums[:, pl.ds(keep_at, quarter), :]
        send_out[j] = sums[:, pl.ds(send_at, quarter), :]


def run_frames(place, counts, pos, obj, halos, pieces, amps, tables, iteration):
    rows, cols = obj.shape[1], obj.shape[2]
    slots, size = amps.shape[1], amps.shape[2]
    vmem = pl.BlockSpec(memory_space=pltpu.VMEM)
    smem = pl.BlockSpec(memory_space=pltpu.SMEM)
    quarter = size // (N_CORE * N_X)
    shapes = [
        jax.ShapeDtypeStruct((2, rows, cols), F32),
        jax.ShapeDtypeStruct((2, size, size), F32),
        jax.ShapeDtypeStruct((2, size, cols - size), BF),
        jax.ShapeDtypeStruct((2, rows, size), BF),
        jax.ShapeDtypeStruct((2, size, size), BF),
        jax.ShapeDtypeStruct((N_X, 3, quarter, size), F32),
        jax.ShapeDtypeStruct((N_X, 3, quarter, size), F32),
        jax.ShapeDtypeStruct((1, 1), F32),
    ]
    scratch = [
        pltpu.VMEM((2, (cols + size) // LANES, rows + size, LANES), F32),
        pltpu.VMEM((2, (cols + size) // LANES, rows + size, LANES), F32),
        pltpu.VMEM((3, size, size), F32),
        pltpu.VMEM((GROUPS[0], 2 * size, size), BF),
        pltpu.VMEM((GROUPS[0], 2 * size, size), BF),
        pltpu.VMEM((GROUPS[0], 2, size, size), F32),
        pltpu.VMEM((slots, size, size), BF),
        pltpu.SemaphoreType.DMA((slots,)),
    ]
    lows, right, corner = halos
    scratch.append(pltpu.SemaphoreType.DMA((4 + len(lows) + len(pieces),)))
    scratch += [pltpu.VMEM(obj.shape, F32), pltpu.VMEM((2, size, cols), BF)]
    scratch += [pltpu.VMEM(value.shape, value.dtype) for value in (right, corner, *pieces, tables)]
    if len(pieces) > 1:
        scratch.append(pltpu.VMEM((2, size, size), F32))
    return pl.pallas_call(
        functools.partial(frames_kernel, iteration, len(lows), len(pieces)),
        out_shape=shapes,
        in_specs=[smem] * 3 + [pl.BlockSpec(memory_space=pltpu.HBM)] * (5 + len(lows) + len(pieces)),
        out_specs=[vmem] * 7 + [smem],
        scratch_shapes=scratch,
        compiler_params=pltpu.CompilerParams(vmem_limit_bytes=44 << 20),
        cost_estimate=pl.CostEstimate(flops=6_000_000_000, bytes_accessed=8_000_000, transcendentals=0),
        name="frames",
    )(place, counts, pos, obj, *lows, right, corner, *pieces, amps, tables)


def spec(space):
    return pl.BlockSpec(memory_space=space)


def small_call(body, shapes, operands, name, limit=16):
    spaces = [pltpu.SMEM if v.size <= 2 else pltpu.VMEM for v in operands[0]] + [pl.ANY] * len(operands[1])
    return pl.pallas_call(
        body,
        out_shape=shapes,
        in_specs=[spec(space) for space in spaces],
        out_specs=[spec(pltpu.VMEM)] * len(shapes),
        compiler_params=pltpu.CompilerParams(vmem_limit_bytes=limit << 20),
        cost_estimate=pl.CostEstimate(flops=2_000_000, bytes_accessed=4_000_000, transcendentals=0),
        name=name,
    )(*operands[0], *operands[1])


def x_kernel(a, b, c, d, low_left, low_right, corner, total, down):
    size = low_left.shape[2]
    total[...] = a[0] + b[...] + c[...] + d[...]
    down[:, :, :size] = (low_left[...] + corner[...].astype(F32)).astype(BF)
    down[:, :, size:] = low_right[...]


def y_kernel(a, b, c, d, waited, total):
    total[...] = a[...] + b[...] + c[...] + d[...]


def probe_step(a, b, c, d, mine, fresh):
    total = a[...] + b[...] + c[...] + d[...]
    fresh[...] = mine[...] - total[:2] / (total[2:] + 1.0)


def z_kernel(a, b, c, d, mine, waited, fresh):
    probe_step(a, b, c, d, mine, fresh)


def object_step(obj, own, left, down, step, obj_out):
    size = left.shape[2]
    alpha = step[0, 0]
    obj_out[:, :, :size] = obj[:, :, :size] - alpha * (own[:, :, :size] + left[...].astype(F32))
    obj_out[:, :size, :size] -= alpha * down[:, :, :size].astype(F32)
    obj_out[:, :size, size:] = obj[:, :size, size:] - alpha * (own[:, :size, size:] + down[:, :, size:].astype(F32))
    obj_out[:, size:, size:] = obj[:, size:, size:] - alpha * own[:, size:, size:]


def both_kernel(a, b, c, d, mine, obj, own, left, down, step, fresh, obj_out, below, right):
    probe_step(a, b, c, d, mine, fresh)
    object_step(obj, own, left, down, step, obj_out)
    size = left.shape[2]
    below[...] = obj_out[:, :size, :].astype(BF)
    right[...] = obj_out[:, :, :size].astype(BF)


def probe_kernel(place, mine, other, out):
    core, x = place[0], place[1]
    size = out.shape[1]
    half, quarter = size // N_CORE, size // (N_CORE * N_X)
    for piece, side in ((mine, core), (other, 1 - core)):
        for j in range(N_X):
            at = pl.multiple_of(side * half + lax.rem(x - j + N_X, N_X) * quarter, quarter)
            out[:, pl.ds(at, quarter), :] = piece[j]


def run_probe(place, mine, other):
    vmem = pl.BlockSpec(memory_space=pltpu.VMEM)
    size = mine.shape[-1]
    return pl.pallas_call(
        probe_kernel,
        out_shape=jax.ShapeDtypeStruct((2, size, size), F32),
        in_specs=[pl.BlockSpec(memory_space=pltpu.SMEM), vmem, vmem],
        out_specs=vmem,
        name="probe_whole",
    )(place, mine, other)


def moved(value, axis, count, steps):
    first, last = max(0, -steps), min(count, count - steps)
    return lax.ppermute(value, axis, [(s, s + steps) for s in range(first, last)])


def turned(value, axis, steps):
    return lax.ppermute(value, axis, [(s, (s + steps) % 4) for s in range(4)])


def swapped(value):
    return lax.ppermute(value, "core", [(0, 1), (1, 0)])


def halo(lows, right):
    size = right.shape[2]
    first = moved(lows[0], ROW, N_ROW, -1)
    right = moved(right, COL, N_COL, -1)
    others = [moved(low, ROW, N_ROW, -1) for low in lows[1:]]
    corner = moved(first[:, :, :size], COL, N_COL, -1)
    return ((first, *others), right, corner)


def around(value, axis):
    return [value] + [turned(value, axis, j) for j in (1, 2, 3)]


def local(tables, obj, probe, amps, positions, counts):
    rows, cols = obj.shape[1], obj.shape[2]
    size = probe.shape[-1]
    half, quarter = size // N_CORE, size // (N_CORE * N_X)
    core, x = lax.axis_index("core"), lax.axis_index("x")
    place = jnp.stack([core, x]).astype(jnp.int32)
    mine = lax.dynamic_slice(probe, (0, core * half + x * quarter, 0), (2, quarter, size))
    whole = jax.ShapeDtypeStruct(obj.shape, F32)
    flat = jax.ShapeDtypeStruct((2, size, cols), BF)
    tall = jax.ShapeDtypeStruct((2, rows, size), BF)
    share = jax.ShapeDtypeStruct((3, quarter, size), F32)
    part = jax.ShapeDtypeStruct(mine.shape, F32)
    lows = [obj[:, :size, :size].astype(BF), obj[:, :size, size:].astype(BF)]
    right = obj[:, :, :size].astype(BF)
    pieces = (probe,)
    for iteration in range(ITERS):
        halos = halo(lows, right)
        own, low_left, low_right, right, corner, keep, send, step = run_frames(
            place, counts[iteration, 0], positions[iteration], obj, halos, pieces, amps, tables, iteration
        )
        corner = moved(corner, COL, N_COL, 1)
        left = moved(right, COL, N_COL, 1)
        sums = keep + swapped(send)
        sums = [sums[:1]] + [turned(sums[j], "x", j) for j in (1, 2, 3)]
        total, down = small_call(x_kernel, [share, flat], ([*sums, low_left, low_right, corner], []), "x_sum")
        down = moved(down, ROW, N_ROW, 1)
        (total,) = small_call(y_kernel, [share], (around(total, "y"), [left]), "y_sum")
        sums = around(total, "z") + [mine]
        if iteration < ITERS - 1:
            mine, obj, *lows, right = small_call(
                both_kernel, [part, whole, flat, tall], ([*sums, obj, own, left, down, step], []), "z_sum_object"
            )
        else:
            (mine,) = small_call(z_kernel, [part], (sums, [down]), "z_sum")
            (obj,) = small_call(object_step, [whole], ([obj, own, left, down, step], []), "object_update")
        stack = jnp.stack(around(mine, "x"))
        pieces = (stack, swapped(stack))
    return (obj, run_probe(place, *pieces))


def solution(mesh):
    fine = Mesh(mesh.devices.reshape(N_X, N_Z, N_Y, N_CORE), ("x", "z", "y", "core"))
    placed = (
        P(None, ROW, COL),
        P(),
        P(None, ROW + COL, None, None),
        P(None, None, ROW + COL),
        P(None, COL, ROW),
    )
    blocks = jnp.asarray(chirp_blocks(256))
    return jax.shard_map(
        functools.partial(local, blocks),
        mesh=fine, in_specs=placed, out_specs=(P(None, ROW, COL), P()), check_vma=False,
    )
```

```python
import functools

import jax
import jax.numpy as jnp
import ml_dtypes
import numpy as np
from jax import lax
from jax.experimental import pallas as pl
from jax.experimental.pallas import tpu as pltpu
from jax.sharding import Mesh, PartitionSpec as P

ITERS = 2
FLOOR = 0.3
ALPHA = 0.5
LANES = 128
CHUNK = 32
GROUPS = (6, 2, 1)
N_X, N_Z, N_Y, N_CORE = 4, 4, 4, 2
N_ROW, N_COL = N_X * N_Z, N_Y * N_CORE
ROW, COL = ("x", "z"), ("y", "core")
BF, F32 = jnp.bfloat16, jnp.float32


def chirp_blocks(size):
    offset = np.arange(size, dtype=np.int64)
    units = (offset[:, None] - offset[None, :]) ** 2 % (2 * size)
    phase = np.float32(np.pi) * units.astype(np.float32) / np.float32(size)
    scale = np.float32(1.0 / np.sqrt(size))
    real = (np.cos(phase) * scale).astype(ml_dtypes.bfloat16)
    imag = (np.sin(phase) * scale).astype(ml_dtypes.bfloat16)
    forward = np.block([[real, -imag], [imag, real]])
    return np.stack([forward, forward.T])


def frames_kernel(
    iteration, n_low, n_pieces,
    place, counts, pos, obj, *rest,
):
    lows, (right, corner), rest = rest[:n_low], rest[n_low : n_low + 2], rest[n_low + 2 :]
    pieces, (amps, tables), rest = rest[:n_pieces], rest[n_pieces : n_pieces + 2], rest[n_pieces + 2 :]
    own_out, down_out, right_out, corner_out, keep_out, send_out, step_out = rest[:7]
    ext, acc, sums, wave, mis, patch, levels, arrived, here, *rest = rest[7:]
    landing, probe_scratch = rest[: 5 + n_pieces], rest[5 + n_pieces :]
    count = counts[0]
    low_parts, at = [], 0
    for low in lows:
        low_parts.append(landing[1].at[:, :, at : at + low.shape[2]])
        at += low.shape[2]
    sources = (obj, right, corner, *lows, *pieces, tables)
    targets = (landing[0], *landing[2:4], *low_parts, *landing[4:])
    copies = [
        pltpu.make_async_copy(source, target, here.at[i])
        for i, (source, target) in enumerate(zip(sources, targets))
    ]
    for copy in copies:
        copy.start()
    obj, below, right, corner = landing[:4]
    pieces, tables = landing[4 : 4 + n_pieces], landing[4 + n_pieces]
    table_a, table_b = tables.at[0], tables.at[1]

    def fetch(index):
        return pltpu.make_async_copy(amps.at[iteration, index], levels.at[index], arrived.at[index])

    def begin(index, carry):
        fetch(index).start()
        return carry

    lax.fori_loop(0, count, begin, 0)
    rows, cols = obj.shape[1], obj.shape[2]
    size = corner.shape[1]
    row_chunks = size // CHUNK
    inner_tiles, all_tiles = cols // LANES, (cols + size) // LANES
    acc[...] = jnp.zeros_like(acc)
    sums[...] = jnp.zeros_like(sums)
    copies[0].wait()
    for copy in copies[1 : 3 + n_low]:
        copy.wait()
    for j in range(all_tiles):
        inside = j < inner_tiles
        at = (j if inside else j - inner_tiles) * LANES
        upper = obj if inside else right
        ext[:, j, :rows, :] = upper[:, :, at : at + LANES].astype(BF).astype(F32)
        lower = below if inside else corner
        ext[:, j, rows:, :] = lower[:, :, at : at + LANES].astype(F32)
    for copy in copies[3 + n_low :]:
        copy.wait()
    core, x = place[0], place[1]
    half, quarter = size // N_CORE, size // (N_CORE * N_X)
    if n_pieces == 1:
        (probe,) = pieces
    else:
        (probe,) = probe_scratch
        for piece, side in ((pieces[0], core), (pieces[1], 1 - core)):
            for j in range(N_X):
                at = pl.multiple_of(side * half + lax.rem(x - j + N_X, N_X) * quarter, quarter)
                probe[:, pl.ds(at, quarter), :] = piece[j]
    peak = jnp.max(probe[0] * probe[0] + probe[1] * probe[1])
    step_out[0, 0] = ALPHA / (peak + 1e-6)
    lane = lax.broadcasted_iota(jnp.int32, (CHUNK, LANES), 1)

    def frames(indices):
        work = []
        for index in indices:
            fetch(index).wait()
        for slot, index in enumerate(indices):
            top, left = pos[0, index], pos[1, index]
            base = left // LANES
            shift = left - base * LANES
            back_shift = lax.rem(LANES - shift, LANES)
            whole = lane < LANES - shift
            for k in range(row_chunks):
                span = slice(k * CHUNK, (k + 1) * CHUNK)
                parts = []
                for c in range(2):
                    tiles = [
                        pltpu.roll(ext[c, base + j, pl.ds(top + k * CHUNK, CHUNK), :], back_shift, 1)
                        for j in range(3)
                    ]
                    cut = jnp.concatenate(
                        [jnp.where(whole, tiles[0], tiles[1]), jnp.where(whole, tiles[1], tiles[2])], axis=1
                    )
                    patch[slot, c, span, :] = cut
                    parts.append(cut)
                re, im = parts
                pr, pi = probe[0, span, :], probe[1, span, :]
                wave[slot, span, :] = (pr * re - pi * im).astype(BF)
                wave[slot, size + k * CHUNK : size + (k + 1) * CHUNK, :] = (pr * im + pi * re).astype(BF)
                sums[2, span, :] += re * re + im * im
            work.append((index, top, base, shift))
        for slot, (index, top, base, shift) in enumerate(work):
            near = jnp.dot(table_a[...], wave[slot], preferred_element_type=F32).astype(BF)
            near = jnp.concatenate([near[:size], near[size:]], axis=1)
            far = jnp.dot(near, table_b[...], preferred_element_type=F32)
            fr, fi = far[:, :size], far[:, size:]
            scale = lax.rsqrt(jnp.maximum(fr * fr + fi * fi, FLOOR * FLOOR))
            factor = 1.0 - levels[index].astype(F32) * scale
            mis[slot, :size, :] = (fr * factor).astype(BF)
            mis[slot, size:, :] = (fi * factor).astype(BF)
        updates = []
        for slot, _ in enumerate(work):
            back = jnp.dot(table_b[...], mis[slot], preferred_element_type=F32).astype(BF)
            back = jnp.concatenate([back[:size], back[size:]], axis=1)
            updates.append(jnp.dot(back, table_a[...], preferred_element_type=F32))
        for slot, (index, top, base, shift) in enumerate(work):
            update = updates[slot]
            fresh = lane >= shift
            for k in range(row_chunks):
                span = slice(k * CHUNK, (k + 1) * CHUNK)
                ur, ui = update[span, :size], update[span, size:]
                pr, pi = probe[0, span, :], probe[1, span, :]
                re, im = patch[slot, 0, span, :], patch[slot, 1, span, :]
                sums[0, span, :] += re * ur + im * ui
                sums[1, span, :] += re * ui - im * ur
                grads = (pr * ur + pi * ui, pr * ui - pi * ur)
                for c in range(2):
                    grad = grads[c].astype(BF).astype(F32)
                    first = pltpu.roll(grad[:, :LANES], shift, 1)
                    second = pltpu.roll(grad[:, LANES:], shift, 1)
                    pieces = (
                        jnp.where(fresh, first, 0.0),
                        jnp.where(fresh, second, first),
                        jnp.where(fresh, 0.0, second),
                    )
                    for j, piece in enumerate(pieces):
                        acc[c, base + j, pl.ds(top + k * CHUNK, CHUNK), :] += piece

    done = 0
    for group in GROUPS:
        times = (count - done) // group

        def several(index, carry, first=done, group=group):
            frames([first + index * group + i for i in range(group)])
            return carry

        lax.fori_loop(0, times, several, 0)
        done = done + times * group
    for j in range(all_tiles):
        inside = j < inner_tiles
        at = (j if inside else j - inner_tiles) * LANES
        upper = own_out if inside else right_out
        upper[:, :, at : at + LANES] = acc[:, j, :rows, :].astype(upper.dtype)
        lower = down_out if inside else corner_out
        lower[:, :, at : at + LANES] = acc[:, j, rows:, :].astype(lower.dtype)
    for j in range(N_X):
        inner = lax.rem(x + j, N_X) * quarter
        keep_at = pl.multiple_of(core * half + inner, quarter)
        send_at = pl.multiple_of((1 - core) * half + inner, quarter)
        keep_out[j] = sums[:, pl.ds(keep_at, quarter), :]
        send_out[j] = sums[:, pl.ds(send_at, quarter), :]


def run_frames(place, counts, pos, obj, halos, pieces, amps, tables, iteration):
    rows, cols = obj.shape[1], obj.shape[2]
    slots, size = amps.shape[1], amps.shape[2]
    vmem = pl.BlockSpec(memory_space=pltpu.VMEM)
    smem = pl.BlockSpec(memory_space=pltpu.SMEM)
    quarter = size // (N_CORE * N_X)
    shapes = [
        jax.ShapeDtypeStruct((2, rows, cols), F32),
        jax.ShapeDtypeStruct((2, size, cols), BF),
        jax.ShapeDtypeStruct((2, rows, size), BF),
        jax.ShapeDtypeStruct((2, size, size), BF),
        jax.ShapeDtypeStruct((N_X, 3, quarter, size), F32),
        jax.ShapeDtypeStruct((N_X, 3, quarter, size), F32),
        jax.ShapeDtypeStruct((1, 1), F32),
    ]
    scratch = [
        pltpu.VMEM((2, (cols + size) // LANES, rows + size, LANES), F32),
        pltpu.VMEM((2, (cols + size) // LANES, rows + size, LANES), F32),
        pltpu.VMEM((3, size, size), F32),
        pltpu.VMEM((GROUPS[0], 2 * size, size), BF),
        pltpu.VMEM((GROUPS[0], 2 * size, size), BF),
        pltpu.VMEM((GROUPS[0], 2, size, size), F32),
        pltpu.VMEM((slots, size, size), BF),
        pltpu.SemaphoreType.DMA((slots,)),
    ]
    lows, right, corner = halos
    scratch.append(pltpu.SemaphoreType.DMA((4 + len(lows) + len(pieces),)))
    scratch += [pltpu.VMEM(obj.shape, F32), pltpu.VMEM((2, size, cols), BF)]
    scratch += [pltpu.VMEM(value.shape, value.dtype) for value in (right, corner, *pieces, tables)]
    if len(pieces) > 1:
        scratch.append(pltpu.VMEM((2, size, size), F32))
    return pl.pallas_call(
        functools.partial(frames_kernel, iteration, len(lows), len(pieces)),
        out_shape=shapes,
        in_specs=[smem] * 3 + [pl.BlockSpec(memory_space=pltpu.HBM)] * (5 + len(lows) + len(pieces)),
        out_specs=[vmem] * 6 + [smem],
        scratch_shapes=scratch,
        compiler_params=pltpu.CompilerParams(vmem_limit_bytes=48 << 20),
        cost_estimate=pl.CostEstimate(flops=6_000_000_000, bytes_accessed=8_000_000, transcendentals=0),
        name="frames",
    )(place, counts, pos, obj, *lows, right, corner, *pieces, amps, tables)


def spec(space):
    return pl.BlockSpec(memory_space=space)


def small_call(body, shapes, operands, name, limit=16):
    spaces = [pltpu.SMEM if v.size <= 2 else pltpu.VMEM for v in operands[0]] + [pl.ANY] * len(operands[1])
    return pl.pallas_call(
        body,
        out_shape=shapes,
        in_specs=[spec(space) for space in spaces],
        out_specs=[spec(pltpu.VMEM)] * len(shapes),
        compiler_params=pltpu.CompilerParams(vmem_limit_bytes=limit << 20),
        cost_estimate=pl.CostEstimate(flops=2_000_000, bytes_accessed=4_000_000, transcendentals=0),
        name=name,
    )(*operands[0], *operands[1])


def sum_kernel(a, b, c, d, *rest):
    total = rest[-1]
    total[...] = a[...].reshape(total.shape) + b[...] + c[...] + d[...]


def probe_step(a, b, c, d, mine, *rest):
    fresh = rest[-1]
    total = a[...] + b[...] + c[...] + d[...]
    fresh[...] = mine[...] - total[:2] / (total[2:] + 1.0)


def stack_kernel(a, b, c, d, *rest):
    for j, chunk in enumerate((a, b, c, d)):
        rest[-1][j] = chunk[...]


def object_step(obj, own, left, down, diag, step, obj_out):
    size = left.shape[2]
    alpha = step[0, 0]
    obj_out[:, :, :size] = obj[:, :, :size] - alpha * (own[:, :, :size] + left[...].astype(F32))
    obj_out[:, :size, :size] -= alpha * (down[:, :, :size].astype(F32) + diag[...].astype(F32))
    obj_out[:, :size, size:] = obj[:, :size, size:] - alpha * (own[:, :size, size:] + down[:, :, size:].astype(F32))
    obj_out[:, size:, size:] = obj[:, size:, size:] - alpha * own[:, size:, size:]


def last_kernel(obj, own, left, down, diag, step, obj_out, done):
    object_step(obj, own, left, down, diag, step, obj_out)
    done[...] = obj_out[0, :8, :LANES]


def both_kernel(a, b, c, d, obj, own, left, down, diag, step, total, obj_out, below, right):
    sum_kernel(a, b, c, d, total)
    object_step(obj, own, left, down, diag, step, obj_out)
    size = left.shape[2]
    below[...] = obj_out[:, :size, :].astype(BF)
    right[...] = obj_out[:, :, :size].astype(BF)


def probe_kernel(place, mine, other, out):
    core, x = place[0], place[1]
    size = out.shape[1]
    half, quarter = size // N_CORE, size // (N_CORE * N_X)
    for piece, side in ((mine, core), (other, 1 - core)):
        for j in range(N_X):
            at = pl.multiple_of(side * half + lax.rem(x - j + N_X, N_X) * quarter, quarter)
            out[:, pl.ds(at, quarter), :] = piece[j]


def run_probe(place, mine, other):
    vmem = pl.BlockSpec(memory_space=pltpu.VMEM)
    size = mine.shape[-1]
    return pl.pallas_call(
        probe_kernel,
        out_shape=jax.ShapeDtypeStruct((2, size, size), F32),
        in_specs=[pl.BlockSpec(memory_space=pltpu.SMEM), vmem, vmem],
        out_specs=vmem,
        name="probe_whole",
    )(place, mine, other)


def moved(value, axis, count, steps):
    first, last = max(0, -steps), min(count, count - steps)
    return lax.ppermute(value, axis, [(s, s + steps) for s in range(first, last)])


def turned(value, axis, steps):
    return lax.ppermute(value, axis, [(s, (s + steps) % 4) for s in range(4)])


def swapped(value):
    return lax.ppermute(value, "core", [(0, 1), (1, 0)])


def moved_both(value, steps):
    pairs = []
    for r in range(N_ROW):
        for c in range(N_COL):
            if 0 <= r + steps < N_ROW and 0 <= c + steps < N_COL:
                pairs.append((r * N_COL + c, (r + steps) * N_COL + c + steps))
    return lax.ppermute(value, ROW + COL, pairs)


def around(value, axis):
    return [value] + [turned(value, axis, j) for j in (1, 2, 3)]


def local(tables, obj, probe, amps, positions, counts):
    rows, cols = obj.shape[1], obj.shape[2]
    size = probe.shape[-1]
    half, quarter = size // N_CORE, size // (N_CORE * N_X)
    core, x = lax.axis_index("core"), lax.axis_index("x")
    place = jnp.stack([core, x]).astype(jnp.int32)
    mine = lax.dynamic_slice(probe, (0, core * half + x * quarter, 0), (2, quarter, size))
    whole = jax.ShapeDtypeStruct(obj.shape, F32)
    flat = jax.ShapeDtypeStruct((2, size, cols), BF)
    tall = jax.ShapeDtypeStruct((2, rows, size), BF)
    share = jax.ShapeDtypeStruct((3, quarter, size), F32)
    part = jax.ShapeDtypeStruct(mine.shape, F32)
    row = jax.ShapeDtypeStruct((8, LANES), F32)
    half_probe = jax.ShapeDtypeStruct((N_X, *mine.shape), F32)
    first = moved(obj[:, :size, :size].astype(BF), ROW, N_ROW, -1)
    beside = moved(obj[:, :, :size].astype(BF), COL, N_COL, -1)
    second = moved(obj[:, :size, size:].astype(BF), ROW, N_ROW, -1)
    halos = ((first, second), beside, moved(first, COL, N_COL, -1))
    pieces = (probe,)
    for iteration in range(ITERS):
        own, down, right, corner, keep, send, step = run_frames(
            place, counts[iteration, 0], positions[iteration], obj, halos, pieces, amps, tables, iteration
        )
        rims = [moved(right, COL, N_COL, 1), moved(down, ROW, N_ROW, 1), moved_both(corner, 1)]
        sums = keep + swapped(send)
        sums = [sums[:1]] + [turned(sums[j], "x", j) for j in (1, 2, 3)]
        (total,) = small_call(sum_kernel, [share], (sums, []), "x_sum")
        sums = around(total, "y")
        if iteration < ITERS - 1:
            total, obj, below, right = small_call(
                both_kernel, [share, whole, flat, tall], ([*sums, obj, own, *rims, step], []), "y_sum_object"
            )
            below, right = moved(below, ROW, N_ROW, -1), moved(right, COL, N_COL, -1)
            corner = moved(below[:, :, :size], COL, N_COL, -1)
            halos, waited = ((below,), right, corner), [corner]
            (mine,) = small_call(probe_step, [part], ([*around(total, "z"), mine], [below]), "z_sum")
        else:
            (total,) = small_call(sum_kernel, [share], (sums, rims), "y_sum")
            obj, done = small_call(last_kernel, [whole, row], ([obj, own, *rims, step], []), "object_update")
            (mine,) = small_call(probe_step, [part], ([*around(total, "z"), mine], []), "z_sum")
            waited = [done]
        (stack,) = small_call(stack_kernel, [half_probe], (around(mine, "x"), waited), "half_probe")
        pieces = (stack, swapped(stack))
    return (obj, run_probe(place, *pieces))


def solution(mesh):
    fine = Mesh(mesh.devices.reshape(N_X, N_Z, N_Y, N_CORE), ("x", "z", "y", "core"))
    placed = (
        P(None, ROW, COL),
        P(),
        P(None, ROW + COL, None, None),
        P(None, None, ROW + COL),
        P(None, COL, ROW),
    )
    blocks = jnp.asarray(chirp_blocks(256))
    return jax.shard_map(
        functools.partial(local, blocks),
        mesh=fine, in_specs=placed, out_specs=(P(None, ROW, COL), P()), check_vma=False,
    )
```

```python
import functools

import jax
import jax.numpy as jnp
import ml_dtypes
import numpy as np
from jax import lax
from jax.experimental import pallas as pl
from jax.experimental.pallas import tpu as pltpu
from jax.sharding import Mesh, PartitionSpec as P

ITERS = 2
FLOOR = 0.3
ALPHA = 0.5
LANES = 128
CHUNK = 32
GROUPS = (6, 2, 1)
N_X, N_Z, N_Y, N_CORE = 4, 4, 4, 2
N_ROW, N_COL = N_X * N_Z, N_Y * N_CORE
ROW, COL = ("x", "z"), ("y", "core")
BF, F32 = jnp.bfloat16, jnp.float32


def chirp_blocks(size):
    offset = np.arange(size, dtype=np.int64)
    units = (offset[:, None] - offset[None, :]) ** 2 % (2 * size)
    phase = np.float32(np.pi) * units.astype(np.float32) / np.float32(size)
    scale = np.float32(1.0 / np.sqrt(size))
    real = (np.cos(phase) * scale).astype(ml_dtypes.bfloat16)
    imag = (np.sin(phase) * scale).astype(ml_dtypes.bfloat16)
    forward = np.block([[real, -imag], [imag, real]])
    return np.stack([forward, forward.T])


def frames_kernel(
    iteration, n_low, n_pieces,
    place, counts, pos, obj, *rest,
):
    lows, (right, corner), rest = rest[:n_low], rest[n_low : n_low + 2], rest[n_low + 2 :]
    pieces, (amps, tables), rest = rest[:n_pieces], rest[n_pieces : n_pieces + 2], rest[n_pieces + 2 :]
    own_out, low_left, low_right, right_out, corner_out, keep_out, send_out, step_out = rest[:8]
    ext, acc, sums, wave, mis, patch, levels, arrived, here, *rest = rest[8:]
    landing, probe_scratch = rest[: 5 + n_pieces], rest[5 + n_pieces :]
    count = counts[0]
    low_parts, at = [], 0
    for low in lows:
        low_parts.append(landing[1].at[:, :, at : at + low.shape[2]])
        at += low.shape[2]
    sources = (obj, right, corner, *lows, *pieces, tables)
    targets = (landing[0], *landing[2:4], *low_parts, *landing[4:])
    copies = [
        pltpu.make_async_copy(source, target, here.at[i])
        for i, (source, target) in enumerate(zip(sources, targets))
    ]
    for copy in copies:
        copy.start()
    obj, below, right, corner = landing[:4]
    pieces, tables = landing[4 : 4 + n_pieces], landing[4 + n_pieces]
    table_a, table_b = tables.at[0], tables.at[1]

    def fetch(index):
        return pltpu.make_async_copy(amps.at[iteration, index], levels.at[index], arrived.at[index])

    def begin(index, carry):
        fetch(index).start()
        return carry

    lax.fori_loop(0, count, begin, 0)
    rows, cols = obj.shape[1], obj.shape[2]
    size = corner.shape[1]
    row_chunks = size // CHUNK
    inner_tiles, all_tiles, left_tiles = cols // LANES, (cols + size) // LANES, size // LANES
    acc[...] = jnp.zeros_like(acc)
    sums[...] = jnp.zeros_like(sums)
    copies[0].wait()
    for copy in copies[1 : 3 + n_low]:
        copy.wait()
    for j in range(all_tiles):
        inside = j < inner_tiles
        at = (j if inside else j - inner_tiles) * LANES
        upper = obj if inside else right
        ext[:, j, :rows, :] = upper[:, :, at : at + LANES].astype(BF).astype(F32)
        lower = below if inside else corner
        ext[:, j, rows:, :] = lower[:, :, at : at + LANES].astype(F32)
    for copy in copies[3 + n_low :]:
        copy.wait()
    core, x = place[0], place[1]
    half, quarter = size // N_CORE, size // (N_CORE * N_X)
    if n_pieces == 1:
        (probe,) = pieces
    else:
        (probe,) = probe_scratch
        for piece, side in ((pieces[0], core), (pieces[1], 1 - core)):
            for j in range(N_X):
                at = pl.multiple_of(side * half + lax.rem(x - j + N_X, N_X) * quarter, quarter)
                probe[:, pl.ds(at, quarter), :] = piece[j]
    peak = jnp.max(probe[0] * probe[0] + probe[1] * probe[1])
    step_out[0, 0] = ALPHA / (peak + 1e-6)
    lane = lax.broadcasted_iota(jnp.int32, (CHUNK, LANES), 1)

    def frames(indices):
        work = []
        for index in indices:
            fetch(index).wait()
        for slot, index in enumerate(indices):
            top, left = pos[0, index], pos[1, index]
            base = left // LANES
            shift = left - base * LANES
            back_shift = lax.rem(LANES - shift, LANES)
            whole = lane < LANES - shift
            for k in range(row_chunks):
                span = slice(k * CHUNK, (k + 1) * CHUNK)
                parts = []
                for c in range(2):
                    tiles = [
                        pltpu.roll(ext[c, base + j, pl.ds(top + k * CHUNK, CHUNK), :], back_shift, 1)
                        for j in range(3)
                    ]
                    cut = jnp.concatenate(
                        [jnp.where(whole, tiles[0], tiles[1]), jnp.where(whole, tiles[1], tiles[2])], axis=1
                    )
                    patch[slot, c, span, :] = cut
                    parts.append(cut)
                re, im = parts
                pr, pi = probe[0, span, :], probe[1, span, :]
                wave[slot, span, :] = (pr * re - pi * im).astype(BF)
                wave[slot, size + k * CHUNK : size + (k + 1) * CHUNK, :] = (pr * im + pi * re).astype(BF)
                sums[2, span, :] += re * re + im * im
            work.append((index, top, base, shift))
        for slot, (index, top, base, shift) in enumerate(work):
            near = jnp.dot(table_a[...], wave[slot], preferred_element_type=F32).astype(BF)
            near = jnp.concatenate([near[:size], near[size:]], axis=1)
            far = jnp.dot(near, table_b[...], preferred_element_type=F32)
            fr, fi = far[:, :size], far[:, size:]
            scale = lax.rsqrt(jnp.maximum(fr * fr + fi * fi, FLOOR * FLOOR))
            factor = 1.0 - levels[index].astype(F32) * scale
            mis[slot, :size, :] = (fr * factor).astype(BF)
            mis[slot, size:, :] = (fi * factor).astype(BF)
        updates = []
        for slot, _ in enumerate(work):
            back = jnp.dot(table_b[...], mis[slot], preferred_element_type=F32).astype(BF)
            back = jnp.concatenate([back[:size], back[size:]], axis=1)
            updates.append(jnp.dot(back, table_a[...], preferred_element_type=F32))
        for slot, (index, top, base, shift) in enumerate(work):
            update = updates[slot]
            fresh = lane >= shift
            for k in range(row_chunks):
                span = slice(k * CHUNK, (k + 1) * CHUNK)
                ur, ui = update[span, :size], update[span, size:]
                pr, pi = probe[0, span, :], probe[1, span, :]
                re, im = patch[slot, 0, span, :], patch[slot, 1, span, :]
                sums[0, span, :] += re * ur + im * ui
                sums[1, span, :] += re * ui - im * ur
                grads = (pr * ur + pi * ui, pr * ui - pi * ur)
                for c in range(2):
                    grad = grads[c].astype(BF).astype(F32)
                    first = pltpu.roll(grad[:, :LANES], shift, 1)
                    second = pltpu.roll(grad[:, LANES:], shift, 1)
                    pieces = (
                        jnp.where(fresh, first, 0.0),
                        jnp.where(fresh, second, first),
                        jnp.where(fresh, 0.0, second),
                    )
                    for j, piece in enumerate(pieces):
                        acc[c, base + j, pl.ds(top + k * CHUNK, CHUNK), :] += piece

    done = 0
    for group in GROUPS:
        times = (count - done) // group

        def several(index, carry, first=done, group=group):
            frames([first + index * group + i for i in range(group)])
            return carry

        lax.fori_loop(0, times, several, 0)
        done = done + times * group
    for j in range(all_tiles):
        inside = j < inner_tiles
        at = (j if inside else j - inner_tiles) * LANES
        upper = own_out if inside else right_out
        upper[:, :, at : at + LANES] = acc[:, j, :rows, :].astype(upper.dtype)
        lower = (low_left if j < left_tiles else low_right) if inside else corner_out
        at = at if j < left_tiles or not inside else at - size
        lower[:, :, at : at + LANES] = acc[:, j, rows:, :].astype(lower.dtype)
    for j in range(N_X):
        inner = lax.rem(x + j, N_X) * quarter
        keep_at = pl.multiple_of(core * half + inner, quarter)
        send_at = pl.multiple_of((1 - core) * half + inner, quarter)
        keep_out[j] = sums[:, pl.ds(keep_at, quarter), :]
        send_out[j] = sums[:, pl.ds(send_at, quarter), :]


def run_frames(place, counts, pos, obj, halos, pieces, amps, tables, iteration):
    rows, cols = obj.shape[1], obj.shape[2]
    slots, size = amps.shape[1], amps.shape[2]
    vmem = pl.BlockSpec(memory_space=pltpu.VMEM)
    smem = pl.BlockSpec(memory_space=pltpu.SMEM)
    quarter = size // (N_CORE * N_X)
    shapes = [
        jax.ShapeDtypeStruct((2, rows, cols), F32),
        jax.ShapeDtypeStruct((2, size, size), F32),
        jax.ShapeDtypeStruct((2, size, cols - size), BF),
        jax.ShapeDtypeStruct((2, rows, size), BF),
        jax.ShapeDtypeStruct((2, size, size), BF),
        jax.ShapeDtypeStruct((N_X, 3, quarter, size), F32),
        jax.ShapeDtypeStruct((N_X, 3, quarter, size), F32),
        jax.ShapeDtypeStruct((1, 1), F32),
    ]
    scratch = [
        pltpu.VMEM((2, (cols + size) // LANES, rows + size, LANES), F32),
        pltpu.VMEM((2, (cols + size) // LANES, rows + size, LANES), F32),
        pltpu.VMEM((3, size, size), F32),
        pltpu.VMEM((GROUPS[0], 2 * size, size), BF),
        pltpu.VMEM((GROUPS[0], 2 * size, size), BF),
        pltpu.VMEM((GROUPS[0], 2, size, size), F32),
        pltpu.VMEM((slots, size, size), BF),
        pltpu.SemaphoreType.DMA((slots,)),
    ]
    lows, right, corner = halos
    scratch.append(pltpu.SemaphoreType.DMA((4 + len(lows) + len(pieces),)))
    scratch += [pltpu.VMEM(obj.shape, F32), pltpu.VMEM((2, size, cols), BF)]
    scratch += [pltpu.VMEM(value.shape, value.dtype) for value in (right, corner, *pieces, tables)]
    if len(pieces) > 1:
        scratch.append(pltpu.VMEM((2, size, size), F32))
    return pl.pallas_call(
        functools.partial(frames_kernel, iteration, len(lows), len(pieces)),
        out_shape=shapes,
        in_specs=[smem] * 3 + [pl.BlockSpec(memory_space=pltpu.HBM)] * (5 + len(lows) + len(pieces)),
        out_specs=[vmem] * 7 + [smem],
        scratch_shapes=scratch,
        compiler_params=pltpu.CompilerParams(vmem_limit_bytes=44 << 20),
        cost_estimate=pl.CostEstimate(flops=6_000_000_000, bytes_accessed=8_000_000, transcendentals=0),
        name="frames",
    )(place, counts, pos, obj, *lows, right, corner, *pieces, amps, tables)


def spec(space):
    return pl.BlockSpec(memory_space=space)


def small_call(body, shapes, operands, name, limit=16):
    spaces = [pltpu.SMEM if v.size <= 2 else pltpu.VMEM for v in operands[0]] + [pl.ANY] * len(operands[1])
    return pl.pallas_call(
        body,
        out_shape=shapes,
        in_specs=[spec(space) for space in spaces],
        out_specs=[spec(pltpu.VMEM)] * len(shapes),
        compiler_params=pltpu.CompilerParams(vmem_limit_bytes=limit << 20),
        cost_estimate=pl.CostEstimate(flops=2_000_000, bytes_accessed=4_000_000, transcendentals=0),
        name=name,
    )(*operands[0], *operands[1])


def x_kernel(a, b, c, d, low_left, low_right, corner, total, down):
    size = low_left.shape[2]
    total[...] = a[0] + b[...] + c[...] + d[...]
    down[:, :, :size] = (low_left[...] + corner[...].astype(F32)).astype(BF)
    down[:, :, size:] = low_right[...]


def y_kernel(a, b, c, d, waited, total):
    total[...] = a[...] + b[...] + c[...] + d[...]


def probe_step(a, b, c, d, mine, fresh):
    total = a[...] + b[...] + c[...] + d[...]
    fresh[...] = mine[...] - total[:2] / (total[2:] + 1.0)


def z_kernel(a, b, c, d, mine, waited, fresh):
    probe_step(a, b, c, d, mine, fresh)


def object_step(obj, own, left, down, step, obj_out):
    size = left.shape[2]
    alpha = step[0, 0]
    obj_out[:, :, :size] = obj[:, :, :size] - alpha * (own[:, :, :size] + left[...].astype(F32))
    obj_out[:, :size, :size] -= alpha * down[:, :, :size].astype(F32)
    obj_out[:, :size, size:] = obj[:, :size, size:] - alpha * (own[:, :size, size:] + down[:, :, size:].astype(F32))
    obj_out[:, size:, size:] = obj[:, size:, size:] - alpha * own[:, size:, size:]


def last_kernel(obj, own, left, down, step, obj_out, done):
    object_step(obj, own, left, down, step, obj_out)
    done[...] = obj_out[0, :8, :LANES]


def stack_kernel(a, b, c, d, *rest):
    for j, chunk in enumerate((a, b, c, d)):
        rest[-1][j] = chunk[...]


def both_kernel(a, b, c, d, mine, obj, own, left, down, step, fresh, obj_out, below, right):
    probe_step(a, b, c, d, mine, fresh)
    object_step(obj, own, left, down, step, obj_out)
    size = left.shape[2]
    below[...] = obj_out[:, :size, :].astype(BF)
    right[...] = obj_out[:, :, :size].astype(BF)


def probe_kernel(place, mine, other, out):
    core, x = place[0], place[1]
    size = out.shape[1]
    half, quarter = size // N_CORE, size // (N_CORE * N_X)
    for piece, side in ((mine, core), (other, 1 - core)):
        for j in range(N_X):
            at = pl.multiple_of(side * half + lax.rem(x - j + N_X, N_X) * quarter, quarter)
            out[:, pl.ds(at, quarter), :] = piece[j]


def moved(value, axis, count, steps):
    first, last = max(0, -steps), min(count, count - steps)
    return lax.ppermute(value, axis, [(s, s + steps) for s in range(first, last)])


def turned(value, axis, steps):
    return lax.ppermute(value, axis, [(s, (s + steps) % 4) for s in range(4)])


def swapped(value):
    return lax.ppermute(value, "core", [(0, 1), (1, 0)])


def halo(lows, right):
    size = right.shape[2]
    first = moved(lows[0], ROW, N_ROW, -1)
    right = moved(right, COL, N_COL, -1)
    others = [moved(low, ROW, N_ROW, -1) for low in lows[1:]]
    corner = moved(first[:, :, :size], COL, N_COL, -1)
    return ((first, *others), right, corner)


def around(value, axis):
    return [value] + [turned(value, axis, j) for j in (1, 2, 3)]


def local(tables, obj, probe, amps, positions, counts):
    rows, cols = obj.shape[1], obj.shape[2]
    size = probe.shape[-1]
    half, quarter = size // N_CORE, size // (N_CORE * N_X)
    core, x = lax.axis_index("core"), lax.axis_index("x")
    place = jnp.stack([core, x]).astype(jnp.int32)
    mine = lax.dynamic_slice(probe, (0, core * half + x * quarter, 0), (2, quarter, size))
    whole = jax.ShapeDtypeStruct(obj.shape, F32)
    flat = jax.ShapeDtypeStruct((2, size, cols), BF)
    tall = jax.ShapeDtypeStruct((2, rows, size), BF)
    share = jax.ShapeDtypeStruct((3, quarter, size), F32)
    part = jax.ShapeDtypeStruct(mine.shape, F32)
    lows = [obj[:, :size, :size].astype(BF), obj[:, :size, size:].astype(BF)]
    right = obj[:, :, :size].astype(BF)
    pieces = (probe,)
    row = jax.ShapeDtypeStruct((8, LANES), F32)
    half_probe = jax.ShapeDtypeStruct((N_X, *mine.shape), F32)
    halos = halo(lows, right)
    for iteration in range(ITERS):
        own, low_left, low_right, right, corner, keep, send, step = run_frames(
            place, counts[iteration, 0], positions[iteration], obj, halos, pieces, amps, tables, iteration
        )
        corner = moved(corner, COL, N_COL, 1)
        left = moved(right, COL, N_COL, 1)
        sums = keep + swapped(send)
        sums = [sums[:1]] + [turned(sums[j], "x", j) for j in (1, 2, 3)]
        total, down = small_call(x_kernel, [share, flat], ([*sums, low_left, low_right, corner], []), "x_sum")
        down = moved(down, ROW, N_ROW, 1)
        (total,) = small_call(y_kernel, [share], (around(total, "y"), [left]), "y_sum")
        sums = around(total, "z") + [mine]
        if iteration < ITERS - 1:
            mine, obj, below, right = small_call(
                both_kernel, [part, whole, flat, tall], ([*sums, obj, own, left, down, step], []), "z_sum_object"
            )
            halos = halo([below], right)
            waited = [halos[2]]
        else:
            (mine,) = small_call(z_kernel, [part], (sums, [down]), "z_sum")
            obj, done = small_call(last_kernel, [whole, row], ([obj, own, left, down, step], []), "object_update")
            waited = [done]
        (stack,) = small_call(stack_kernel, [half_probe], (around(mine, "x"), waited), "half_probe")
        pieces = (stack, swapped(stack))
    shape = jax.ShapeDtypeStruct((2, size, size), F32)
    (probe,) = small_call(probe_kernel, [shape], ([place, *pieces], []), "probe_whole")
    return (obj, probe)


def solution(mesh):
    fine = Mesh(mesh.devices.reshape(N_X, N_Z, N_Y, N_CORE), ("x", "z", "y", "core"))
    placed = (
        P(None, ROW, COL),
        P(),
        P(None, ROW + COL, None, None),
        P(None, None, ROW + COL),
        P(None, COL, ROW),
    )
    blocks = jnp.asarray(chirp_blocks(256))
    return jax.shard_map(
        functools.partial(local, blocks),
        mesh=fine, in_specs=placed, out_specs=(P(None, ROW, COL), P()), check_vma=False,
    )
```

```python
import functools

import jax
import jax.numpy as jnp
import ml_dtypes
import numpy as np
from jax import lax
from jax.experimental import pallas as pl
from jax.experimental.pallas import tpu as pltpu
from jax.sharding import Mesh, PartitionSpec as P

ITERS = 2
FLOOR = 0.3
ALPHA = 0.5
LANES = 128
CHUNK = 32
GROUPS = (6, 2, 1)
N_X, N_Z, N_Y, N_CORE = 4, 4, 4, 2
N_ROW, N_COL = N_X * N_Z, N_Y * N_CORE
ROW, COL = ("x", "z"), ("y", "core")
BF, F32 = jnp.bfloat16, jnp.float32


def chirp_blocks(size):
    offset = np.arange(size, dtype=np.int64)
    units = (offset[:, None] - offset[None, :]) ** 2 % (2 * size)
    phase = np.float32(np.pi) * units.astype(np.float32) / np.float32(size)
    scale = np.float32(1.0 / np.sqrt(size))
    real = (np.cos(phase) * scale).astype(ml_dtypes.bfloat16)
    imag = (np.sin(phase) * scale).astype(ml_dtypes.bfloat16)
    forward = np.block([[real, -imag], [imag, real]])
    return np.stack([forward, forward.T])


def frames_kernel(
    middle, iteration, n_low, n_pieces,
    place, counts, pos, obj, *rest,
):
    lows, (right, corner), rest = rest[:n_low], rest[n_low : n_low + 2], rest[n_low + 2 :]
    pieces, (amps, tables), rest = rest[:n_pieces], rest[n_pieces : n_pieces + 2], rest[n_pieces + 2 :]
    n_grads = 3 if middle else 5
    grads_out, (keep_out, send_out, step_out) = rest[:n_grads], rest[n_grads : n_grads + 3]
    ext, acc, sums, wave, mis, patch, levels, arrived, here, *rest = rest[n_grads + 3 :]
    landing, probe_scratch = rest[: 5 + n_pieces], rest[5 + n_pieces :]
    count = counts[0]
    low_parts, at = [], 0
    for low in lows:
        low_parts.append(landing[1].at[:, :, at : at + low.shape[2]])
        at += low.shape[2]
    sources = (obj, right, corner, *lows, *pieces, tables)
    targets = (landing[0], *landing[2:4], *low_parts, *landing[4:])
    copies = [
        pltpu.make_async_copy(source, target, here.at[i])
        for i, (source, target) in enumerate(zip(sources, targets))
    ]
    for copy in copies:
        copy.start()
    obj, below, right, corner = landing[:4]
    pieces, tables = landing[4 : 4 + n_pieces], landing[4 + n_pieces]
    table_a, table_b = tables.at[0], tables.at[1]

    def fetch(index):
        return pltpu.make_async_copy(amps.at[iteration, index], levels.at[index], arrived.at[index])

    def begin(index, carry):
        fetch(index).start()
        return carry

    lax.fori_loop(0, count, begin, 0)
    rows, cols = obj.shape[1], obj.shape[2]
    size = corner.shape[1]
    row_chunks = size // CHUNK
    inner_tiles, all_tiles, left_tiles = cols // LANES, (cols + size) // LANES, size // LANES
    acc[...] = jnp.zeros_like(acc)
    sums[...] = jnp.zeros_like(sums)
    copies[0].wait()
    for copy in copies[1 : 3 + n_low]:
        copy.wait()
    for j in range(all_tiles):
        inside = j < inner_tiles
        at = (j if inside else j - inner_tiles) * LANES
        upper = obj if inside else right
        ext[:, j, :rows, :] = upper[:, :, at : at + LANES].astype(BF).astype(F32)
        lower = below if inside else corner
        ext[:, j, rows:, :] = lower[:, :, at : at + LANES].astype(F32)
    for copy in copies[3 + n_low :]:
        copy.wait()
    core, x = place[0], place[1]
    half, quarter = size // N_CORE, size // (N_CORE * N_X)
    if n_pieces == 1:
        (probe,) = pieces
    else:
        (probe,) = probe_scratch
        for piece, side in ((pieces[0], core), (pieces[1], 1 - core)):
            for j in range(N_X):
                at = pl.multiple_of(side * half + lax.rem(x - j + N_X, N_X) * quarter, quarter)
                probe[:, pl.ds(at, quarter), :] = piece[j]
    peak = jnp.max(probe[0] * probe[0] + probe[1] * probe[1])
    step_out[0, 0] = ALPHA / (peak + 1e-6)
    lane = lax.broadcasted_iota(jnp.int32, (CHUNK, LANES), 1)

    def frames(indices):
        work = []
        for index in indices:
            fetch(index).wait()
        for slot, index in enumerate(indices):
            top, left = pos[0, index], pos[1, index]
            base = left // LANES
            shift = left - base * LANES
            back_shift = lax.rem(LANES - shift, LANES)
            whole = lane < LANES - shift
            for k in range(row_chunks):
                span = slice(k * CHUNK, (k + 1) * CHUNK)
                parts = []
                for c in range(2):
                    tiles = [
                        pltpu.roll(ext[c, base + j, pl.ds(top + k * CHUNK, CHUNK), :], back_shift, 1)
                        for j in range(3)
                    ]
                    cut = jnp.concatenate(
                        [jnp.where(whole, tiles[0], tiles[1]), jnp.where(whole, tiles[1], tiles[2])], axis=1
                    )
                    patch[slot, c, span, :] = cut
                    parts.append(cut)
                re, im = parts
                pr, pi = probe[0, span, :], probe[1, span, :]
                wave[slot, span, :] = (pr * re - pi * im).astype(BF)
                wave[slot, size + k * CHUNK : size + (k + 1) * CHUNK, :] = (pr * im + pi * re).astype(BF)
                sums[2, span, :] += re * re + im * im
            work.append((index, top, base, shift))
        for slot, (index, top, base, shift) in enumerate(work):
            near = jnp.dot(table_a[...], wave[slot], preferred_element_type=F32).astype(BF)
            near = jnp.concatenate([near[:size], near[size:]], axis=1)
            far = jnp.dot(near, table_b[...], preferred_element_type=F32)
            fr, fi = far[:, :size], far[:, size:]
            scale = lax.rsqrt(jnp.maximum(fr * fr + fi * fi, FLOOR * FLOOR))
            factor = 1.0 - levels[index].astype(F32) * scale
            mis[slot, :size, :] = (fr * factor).astype(BF)
            mis[slot, size:, :] = (fi * factor).astype(BF)
        updates = []
        for slot, _ in enumerate(work):
            back = jnp.dot(table_b[...], mis[slot], preferred_element_type=F32).astype(BF)
            back = jnp.concatenate([back[:size], back[size:]], axis=1)
            updates.append(jnp.dot(back, table_a[...], preferred_element_type=F32))
        for slot, (index, top, base, shift) in enumerate(work):
            update = updates[slot]
            fresh = lane >= shift
            for k in range(row_chunks):
                span = slice(k * CHUNK, (k + 1) * CHUNK)
                ur, ui = update[span, :size], update[span, size:]
                pr, pi = probe[0, span, :], probe[1, span, :]
                re, im = patch[slot, 0, span, :], patch[slot, 1, span, :]
                sums[0, span, :] += re * ur + im * ui
                sums[1, span, :] += re * ui - im * ur
                grads = (pr * ur + pi * ui, pr * ui - pi * ur)
                for c in range(2):
                    grad = grads[c].astype(BF).astype(F32)
                    first = pltpu.roll(grad[:, :LANES], shift, 1)
                    second = pltpu.roll(grad[:, LANES:], shift, 1)
                    pieces = (
                        jnp.where(fresh, first, 0.0),
                        jnp.where(fresh, second, first),
                        jnp.where(fresh, 0.0, second),
                    )
                    for j, piece in enumerate(pieces):
                        acc[c, base + j, pl.ds(top + k * CHUNK, CHUNK), :] += piece

    done = 0
    for group in GROUPS:
        times = (count - done) // group

        def several(index, carry, first=done, group=group):
            frames([first + index * group + i for i in range(group)])
            return carry

        lax.fori_loop(0, times, several, 0)
        done = done + times * group
    if middle:
        all_out, to_right, to_left = grads_out
        for j in range(all_tiles):
            at = j * LANES
            all_out[:, :, at : at + LANES] = acc[:, j]
            if j < left_tiles:
                to_left[:, :, at : at + LANES] = acc[:, j].astype(BF)
            if j >= inner_tiles:
                at = at - cols
                to_right[:, :, at : at + LANES] = acc[:, j].astype(BF)
    else:
        own_out, low_left, low_right, right_out, corner_out = grads_out
        for j in range(all_tiles):
            inside = j < inner_tiles
            at = (j if inside else j - inner_tiles) * LANES
            upper = own_out if inside else right_out
            upper[:, :, at : at + LANES] = acc[:, j, :rows, :].astype(upper.dtype)
            lower = (low_left if j < left_tiles else low_right) if inside else corner_out
            at = at if j < left_tiles or not inside else at - size
            lower[:, :, at : at + LANES] = acc[:, j, rows:, :].astype(lower.dtype)
    for j in range(N_X):
        inner = lax.rem(x + j, N_X) * quarter
        keep_at = pl.multiple_of(core * half + inner, quarter)
        send_at = pl.multiple_of((1 - core) * half + inner, quarter)
        keep_out[j] = sums[:, pl.ds(keep_at, quarter), :]
        send_out[j] = sums[:, pl.ds(send_at, quarter), :]


def run_frames(place, counts, pos, obj, halos, pieces, amps, tables, iteration, middle):
    rows, cols = obj.shape[1], obj.shape[2]
    slots, size = amps.shape[1], amps.shape[2]
    vmem = pl.BlockSpec(memory_space=pltpu.VMEM)
    smem = pl.BlockSpec(memory_space=pltpu.SMEM)
    quarter = size // (N_CORE * N_X)
    if middle:
        shapes = [
            jax.ShapeDtypeStruct((2, rows + size, cols + size), F32),
            jax.ShapeDtypeStruct((2, rows + size, size), BF),
            jax.ShapeDtypeStruct((2, rows + size, size), BF),
        ]
    else:
        shapes = [
            jax.ShapeDtypeStruct((2, rows, cols), F32),
            jax.ShapeDtypeStruct((2, size, size), F32),
            jax.ShapeDtypeStruct((2, size, cols - size), BF),
            jax.ShapeDtypeStruct((2, rows, size), BF),
            jax.ShapeDtypeStruct((2, size, size), BF),
        ]
    shapes += [
        jax.ShapeDtypeStruct((N_X, 3, quarter, size), F32),
        jax.ShapeDtypeStruct((N_X, 3, quarter, size), F32),
        jax.ShapeDtypeStruct((1, 1), F32),
    ]
    scratch = [
        pltpu.VMEM((2, (cols + size) // LANES, rows + size, LANES), F32),
        pltpu.VMEM((2, (cols + size) // LANES, rows + size, LANES), F32),
        pltpu.VMEM((3, size, size), F32),
        pltpu.VMEM((GROUPS[0], 2 * size, size), BF),
        pltpu.VMEM((GROUPS[0], 2 * size, size), BF),
        pltpu.VMEM((GROUPS[0], 2, size, size), F32),
        pltpu.VMEM((slots, size, size), BF),
        pltpu.SemaphoreType.DMA((slots,)),
    ]
    lows, right, corner = halos
    scratch.append(pltpu.SemaphoreType.DMA((4 + len(lows) + len(pieces),)))
    scratch += [pltpu.VMEM(obj.shape, F32), pltpu.VMEM((2, size, cols), BF)]
    scratch += [pltpu.VMEM(value.shape, value.dtype) for value in (right, corner, *pieces, tables)]
    if len(pieces) > 1:
        scratch.append(pltpu.VMEM((2, size, size), F32))
    return pl.pallas_call(
        functools.partial(frames_kernel, middle, iteration, len(lows), len(pieces)),
        out_shape=shapes,
        in_specs=[smem] * 3 + [pl.BlockSpec(memory_space=pltpu.HBM)] * (5 + len(lows) + len(pieces)),
        out_specs=[vmem] * (len(shapes) - 1) + [smem],
        scratch_shapes=scratch,
        compiler_params=pltpu.CompilerParams(vmem_limit_bytes=44 << 20),
        cost_estimate=pl.CostEstimate(flops=6_000_000_000, bytes_accessed=8_000_000, transcendentals=0),
        name="frames",
    )(place, counts, pos, obj, *lows, right, corner, *pieces, amps, tables)


def spec(space):
    return pl.BlockSpec(memory_space=space)


def small_call(body, shapes, operands, name, limit=16):
    spaces = [pltpu.SMEM if v.size <= 2 else pltpu.VMEM for v in operands[0]] + [pl.ANY] * len(operands[1])
    return pl.pallas_call(
        body,
        out_shape=shapes,
        in_specs=[spec(space) for space in spaces],
        out_specs=[spec(pltpu.VMEM)] * len(shapes),
        compiler_params=pltpu.CompilerParams(vmem_limit_bytes=limit << 20),
        cost_estimate=pl.CostEstimate(flops=2_000_000, bytes_accessed=4_000_000, transcendentals=0),
        name=name,
    )(*operands[0], *operands[1])


def x_kernel(a, b, c, d, low_left, low_right, corner, total, down):
    size = low_left.shape[2]
    total[...] = a[0] + b[...] + c[...] + d[...]
    down[:, :, :size] = (low_left[...] + corner[...].astype(F32)).astype(BF)
    down[:, :, size:] = low_right[...]


def y_kernel(a, b, c, d, waited, total):
    total[...] = a[...] + b[...] + c[...] + d[...]


def probe_step(a, b, c, d, mine, fresh):
    total = a[...] + b[...] + c[...] + d[...]
    fresh[...] = mine[...] - total[:2] / (total[2:] + 1.0)


def z_kernel(a, b, c, d, mine, waited, fresh):
    probe_step(a, b, c, d, mine, fresh)


def object_step(obj, own, left, down, step, obj_out):
    size = left.shape[2]
    alpha = step[0, 0]
    obj_out[:, :, :size] = obj[:, :, :size] - alpha * (own[:, :, :size] + left[...].astype(F32))
    obj_out[:, :size, :size] -= alpha * down[:, :, :size].astype(F32)
    obj_out[:, :size, size:] = obj[:, :size, size:] - alpha * (own[:, :size, size:] + down[:, :, size:].astype(F32))
    obj_out[:, size:, size:] = obj[:, size:, size:] - alpha * own[:, size:, size:]


def last_kernel(obj, own, left, down, step, obj_out, done):
    object_step(obj, own, left, down, step, obj_out)
    done[...] = obj_out[0, :8, :LANES]


def stack_kernel(a, b, c, d, *rest):
    for j, chunk in enumerate((a, b, c, d)):
        rest[-1][j] = chunk[...]


def sum_kernel(a, b, c, d, *rest):
    total = rest[-1]
    total[...] = a[...].reshape(total.shape) + b[...] + c[...] + d[...]


def rim_kernel(a, b, c, d, grads, from_left, from_right, total, down, up):
    sum_kernel(a, b, c, d, total)
    size = down.shape[1]
    cols = grads.shape[2] - size
    rows = grads.shape[1] - size
    for out, span in ((down, slice(rows, rows + size)), (up, slice(0, size))):
        out[:, :, :size] = (grads[:, span, :size] + from_left[:, span].astype(F32)).astype(BF)
        out[:, :, size:cols] = grads[:, span, size:cols].astype(BF)
        out[:, :, cols:] = (grads[:, span, cols:] + from_right[:, span].astype(F32)).astype(BF)


def wide_kernel(
    obj, low_left, low_right, right, corner, grads, from_left, from_right, above, under, step,
    obj_out, below_out, right_out, corner_out,
):
    size = corner.shape[1]
    rows, cols = obj.shape[1], obj.shape[2]
    alpha = step[0, 0]
    for r in (slice(0, size), slice(size, rows), slice(rows, rows + size)):
        for c in (slice(0, size), slice(size, cols), slice(cols, cols + size)):
            outside_r, outside_c = r.start == rows, c.start == cols
            total = grads[:, r, c]
            if c.start == 0:
                total = total + from_left[:, r].astype(F32)
            if outside_c:
                total = total + from_right[:, r].astype(F32)
            if r.start == 0:
                total = total + above[:, :, c].astype(F32)
            if outside_r:
                total = total + under[:, :, c].astype(F32)
            if outside_r and outside_c:
                corner_out[...] = (corner[...].astype(F32) - alpha * total).astype(BF)
            elif outside_r:
                low = low_left if c.start == 0 else low_right
                below_out[:, :, c] = (low[...].astype(F32) - alpha * total).astype(BF)
            elif outside_c:
                right_out[:, r, :] = (right[:, r, :].astype(F32) - alpha * total).astype(BF)
            else:
                obj_out[:, r, c] = obj[:, r, c] - alpha * total


def probe_kernel(place, mine, other, out):
    core, x = place[0], place[1]
    size = out.shape[1]
    half, quarter = size // N_CORE, size // (N_CORE * N_X)
    for piece, side in ((mine, core), (other, 1 - core)):
        for j in range(N_X):
            at = pl.multiple_of(side * half + lax.rem(x - j + N_X, N_X) * quarter, quarter)
            out[:, pl.ds(at, quarter), :] = piece[j]


def moved(value, axis, count, steps):
    first, last = max(0, -steps), min(count, count - steps)
    return lax.ppermute(value, axis, [(s, s + steps) for s in range(first, last)])


def turned(value, axis, steps):
    return lax.ppermute(value, axis, [(s, (s + steps) % 4) for s in range(4)])


def swapped(value):
    return lax.ppermute(value, "core", [(0, 1), (1, 0)])


def halo(lows, right):
    size = right.shape[2]
    first = moved(lows[0], ROW, N_ROW, -1)
    right = moved(right, COL, N_COL, -1)
    others = [moved(low, ROW, N_ROW, -1) for low in lows[1:]]
    corner = moved(first[:, :, :size], COL, N_COL, -1)
    return ((first, *others), right, corner)


def around(value, axis):
    return [value] + [turned(value, axis, j) for j in (1, 2, 3)]


def local(tables, obj, probe, amps, positions, counts):
    rows, cols = obj.shape[1], obj.shape[2]
    size = probe.shape[-1]
    half, quarter = size // N_CORE, size // (N_CORE * N_X)
    core, x = lax.axis_index("core"), lax.axis_index("x")
    place = jnp.stack([core, x]).astype(jnp.int32)
    mine = lax.dynamic_slice(probe, (0, core * half + x * quarter, 0), (2, quarter, size))
    whole = jax.ShapeDtypeStruct(obj.shape, F32)
    flat = jax.ShapeDtypeStruct((2, size, cols), BF)
    tall = jax.ShapeDtypeStruct((2, rows, size), BF)
    share = jax.ShapeDtypeStruct((3, quarter, size), F32)
    part = jax.ShapeDtypeStruct(mine.shape, F32)
    lows = [obj[:, :size, :size].astype(BF), obj[:, :size, size:].astype(BF)]
    right = obj[:, :, :size].astype(BF)
    pieces = (probe,)
    row = jax.ShapeDtypeStruct((8, LANES), F32)
    half_probe = jax.ShapeDtypeStruct((N_X, *mine.shape), F32)
    halos = halo(lows, right)
    square = jax.ShapeDtypeStruct((2, size, size), BF)
    wide = jax.ShapeDtypeStruct((2, size, cols + size), BF)
    for iteration in range(ITERS):
        middle = iteration < ITERS - 1
        *grads, keep, send, step = run_frames(
            place, counts[iteration, 0], positions[iteration], obj, halos, pieces, amps, tables, iteration, middle
        )
        if middle:
            grads, to_right, to_left = grads
            from_left, from_right = moved(to_right, COL, N_COL, 1), moved(to_left, COL, N_COL, -1)
        else:
            own, low_left, low_right, right, corner = grads
            corner = moved(corner, COL, N_COL, 1)
            left = moved(right, COL, N_COL, 1)
        sums = keep + swapped(send)
        sums = [sums[:1]] + [turned(sums[j], "x", j) for j in (1, 2, 3)]
        if middle:
            (total,) = small_call(sum_kernel, [share], (sums, []), "x_sum")
            total, down, up = small_call(
                rim_kernel, [share, wide, wide], ([*around(total, "z"), grads, from_left, from_right], []), "z_sum_rims"
            )
            above, under = moved(down, ROW, N_ROW, 1), moved(up, ROW, N_ROW, -1)
            (mine,) = small_call(probe_step, [part], ([*around(total, "y"), mine], []), "y_sum")
            lows, right, corner = halos
            obj, below, right, corner = small_call(
                wide_kernel,
                [whole, flat, tall, square],
                ([obj, *lows, right, corner, grads, from_left, from_right, above, under, step], []),
                "wide_update",
                24,
            )
            halos, waited = ((below,), right, corner), [above, under]
        else:
            total, down = small_call(x_kernel, [share, flat], ([*sums, low_left, low_right, corner], []), "x_sum")
            down = moved(down, ROW, N_ROW, 1)
            (total,) = small_call(y_kernel, [share], (around(total, "y"), [left]), "y_sum")
            (mine,) = small_call(z_kernel, [part], ([*around(total, "z"), mine], [down]), "z_sum")
            obj, done = small_call(last_kernel, [whole, row], ([obj, own, left, down, step], []), "object_update")
            waited = [done]
        (stack,) = small_call(stack_kernel, [half_probe], (around(mine, "x"), waited), "half_probe")
        pieces = (stack, swapped(stack))
    shape = jax.ShapeDtypeStruct((2, size, size), F32)
    (probe,) = small_call(probe_kernel, [shape], ([place, *pieces], []), "probe_whole")
    return (obj, probe)


def solution(mesh):
    fine = Mesh(mesh.devices.reshape(N_X, N_Z, N_Y, N_CORE), ("x", "z", "y", "core"))
    placed = (
        P(None, ROW, COL),
        P(),
        P(None, ROW + COL, None, None),
        P(None, None, ROW + COL),
        P(None, COL, ROW),
    )
    blocks = jnp.asarray(chirp_blocks(256))
    return jax.shard_map(
        functools.partial(local, blocks),
        mesh=fine, in_specs=placed, out_specs=(P(None, ROW, COL), P()), check_vma=False,
    )
```

```python
import functools

import jax
import jax.numpy as jnp
import ml_dtypes
import numpy as np
from jax import lax
from jax.experimental import pallas as pl
from jax.experimental.pallas import tpu as pltpu
from jax.sharding import Mesh, PartitionSpec as P

ITERS = 2
FLOOR = 0.3
ALPHA = 0.5
LANES = 128
CHUNK = 32
GROUPS = (6, 2, 1)
N_X, N_Z, N_Y, N_CORE = 4, 4, 4, 2
N_ROW, N_COL = N_X * N_Z, N_Y * N_CORE
ROW, COL = ("x", "z"), ("y", "core")
BF, F32 = jnp.bfloat16, jnp.float32


def chirp_blocks(size):
    offset = np.arange(size, dtype=np.int64)
    units = (offset[:, None] - offset[None, :]) ** 2 % (2 * size)
    phase = np.float32(np.pi) * units.astype(np.float32) / np.float32(size)
    scale = np.float32(1.0 / np.sqrt(size))
    real = (np.cos(phase) * scale).astype(ml_dtypes.bfloat16)
    imag = (np.sin(phase) * scale).astype(ml_dtypes.bfloat16)
    forward = np.block([[real, -imag], [imag, real]])
    return np.stack([forward, forward.T])


def frames_kernel(
    middle, iteration, n_low, n_pieces,
    place, counts, pos, obj, *rest,
):
    lows, (right, corner), rest = rest[:n_low], rest[n_low : n_low + 2], rest[n_low + 2 :]
    pieces, (amps, tables), rest = rest[:n_pieces], rest[n_pieces : n_pieces + 2], rest[n_pieces + 2 :]
    n_grads = 3 if middle else 5
    grads_out, (keep_out, send_out, step_out) = rest[:n_grads], rest[n_grads : n_grads + 3]
    ext, acc, sums, wave, mis, patch, levels, arrived, here, *rest = rest[n_grads + 3 :]
    landing, probe_scratch = rest[: 5 + n_pieces], rest[5 + n_pieces :]
    count = counts[0]
    low_parts, at = [], 0
    for low in lows:
        low_parts.append(landing[1].at[:, :, at : at + low.shape[2]])
        at += low.shape[2]
    sources = (obj, right, corner, *lows, *pieces, tables)
    targets = (landing[0], *landing[2:4], *low_parts, *landing[4:])
    copies = [
        pltpu.make_async_copy(source, target, here.at[i])
        for i, (source, target) in enumerate(zip(sources, targets))
    ]
    for copy in copies:
        copy.start()
    obj, below, right, corner = landing[:4]
    pieces, tables = landing[4 : 4 + n_pieces], landing[4 + n_pieces]
    table_a, table_b = tables.at[0], tables.at[1]

    def fetch(index):
        return pltpu.make_async_copy(amps.at[iteration, index], levels.at[index], arrived.at[index])

    def begin(index, carry):
        fetch(index).start()
        return carry

    lax.fori_loop(0, count, begin, 0)
    rows, cols = obj.shape[1], obj.shape[2]
    size = corner.shape[1]
    row_chunks = size // CHUNK
    inner_tiles, all_tiles, left_tiles = cols // LANES, (cols + size) // LANES, size // LANES
    acc[...] = jnp.zeros_like(acc)
    sums[...] = jnp.zeros_like(sums)
    copies[0].wait()
    for copy in copies[1 : 3 + n_low]:
        copy.wait()
    for j in range(all_tiles):
        inside = j < inner_tiles
        at = (j if inside else j - inner_tiles) * LANES
        upper = obj if inside else right
        ext[:, j, :rows, :] = upper[:, :, at : at + LANES].astype(BF).astype(F32)
        lower = below if inside else corner
        ext[:, j, rows:, :] = lower[:, :, at : at + LANES].astype(F32)
    for copy in copies[3 + n_low :]:
        copy.wait()
    core, x = place[0], place[1]
    half, quarter = size // N_CORE, size // (N_CORE * N_X)
    if n_pieces == 1:
        (probe,) = pieces
    else:
        (probe,) = probe_scratch
        for piece, side in ((pieces[0], core), (pieces[1], 1 - core)):
            for j in range(N_X):
                at = pl.multiple_of(side * half + lax.rem(x - j + N_X, N_X) * quarter, quarter)
                probe[:, pl.ds(at, quarter), :] = piece[j]
    peak = jnp.max(probe[0] * probe[0] + probe[1] * probe[1])
    step_out[0, 0] = ALPHA / (peak + 1e-6)
    lane = lax.broadcasted_iota(jnp.int32, (CHUNK, LANES), 1)

    def frames(indices):
        work = []
        for index in indices:
            fetch(index).wait()
        for slot, index in enumerate(indices):
            top, left = pos[0, index], pos[1, index]
            base = left // LANES
            shift = left - base * LANES
            back_shift = lax.rem(LANES - shift, LANES)
            whole = lane < LANES - shift
            for k in range(row_chunks):
                span = slice(k * CHUNK, (k + 1) * CHUNK)
                parts = []
                for c in range(2):
                    tiles = [
                        pltpu.roll(ext[c, base + j, pl.ds(top + k * CHUNK, CHUNK), :], back_shift, 1)
                        for j in range(3)
                    ]
                    cut = jnp.concatenate(
                        [jnp.where(whole, tiles[0], tiles[1]), jnp.where(whole, tiles[1], tiles[2])], axis=1
                    )
                    patch[slot, c, span, :] = cut
                    parts.append(cut)
                re, im = parts
                pr, pi = probe[0, span, :], probe[1, span, :]
                wave[slot, span, :] = (pr * re - pi * im).astype(BF)
                wave[slot, size + k * CHUNK : size + (k + 1) * CHUNK, :] = (pr * im + pi * re).astype(BF)
                sums[2, span, :] += re * re + im * im
            work.append((index, top, base, shift))
        for slot, (index, top, base, shift) in enumerate(work):
            near = jnp.dot(table_a[...], wave[slot], preferred_element_type=F32).astype(BF)
            near = jnp.concatenate([near[:size], near[size:]], axis=1)
            far = jnp.dot(near, table_b[...], preferred_element_type=F32)
            fr, fi = far[:, :size], far[:, size:]
            scale = lax.rsqrt(jnp.maximum(fr * fr + fi * fi, FLOOR * FLOOR))
            factor = 1.0 - levels[index].astype(F32) * scale
            mis[slot, :size, :] = (fr * factor).astype(BF)
            mis[slot, size:, :] = (fi * factor).astype(BF)
        updates = []
        for slot, _ in enumerate(work):
            back = jnp.dot(table_b[...], mis[slot], preferred_element_type=F32).astype(BF)
            back = jnp.concatenate([back[:size], back[size:]], axis=1)
            updates.append(jnp.dot(back, table_a[...], preferred_element_type=F32))
        for slot, (index, top, base, shift) in enumerate(work):
            update = updates[slot]
            fresh = lane >= shift
            for k in range(row_chunks):
                span = slice(k * CHUNK, (k + 1) * CHUNK)
                ur, ui = update[span, :size], update[span, size:]
                pr, pi = probe[0, span, :], probe[1, span, :]
                re, im = patch[slot, 0, span, :], patch[slot, 1, span, :]
                sums[0, span, :] += re * ur + im * ui
                sums[1, span, :] += re * ui - im * ur
                grads = (pr * ur + pi * ui, pr * ui - pi * ur)
                for c in range(2):
                    grad = grads[c].astype(BF).astype(F32)
                    first = pltpu.roll(grad[:, :LANES], shift, 1)
                    second = pltpu.roll(grad[:, LANES:], shift, 1)
                    pieces = (
                        jnp.where(fresh, first, 0.0),
                        jnp.where(fresh, second, first),
                        jnp.where(fresh, 0.0, second),
                    )
                    for j, piece in enumerate(pieces):
                        acc[c, base + j, pl.ds(top + k * CHUNK, CHUNK), :] += piece

    done = 0
    for group in GROUPS:
        times = (count - done) // group

        def several(index, carry, first=done, group=group):
            frames([first + index * group + i for i in range(group)])
            return carry

        lax.fori_loop(0, times, several, 0)
        done = done + times * group
    if middle:
        all_out, to_right, to_left = grads_out
        for j in range(all_tiles):
            at = j * LANES
            all_out[:, :, at : at + LANES] = acc[:, j]
            if j < left_tiles:
                to_left[:, :, at : at + LANES] = acc[:, j].astype(BF)
            if j >= inner_tiles:
                at = at - cols
                to_right[:, :, at : at + LANES] = acc[:, j].astype(BF)
    else:
        own_out, low_left, low_right, right_out, corner_out = grads_out
        for j in range(all_tiles):
            inside = j < inner_tiles
            at = (j if inside else j - inner_tiles) * LANES
            upper = own_out if inside else right_out
            upper[:, :, at : at + LANES] = acc[:, j, :rows, :].astype(upper.dtype)
            lower = (low_left if j < left_tiles else low_right) if inside else corner_out
            at = at if j < left_tiles or not inside else at - size
            lower[:, :, at : at + LANES] = acc[:, j, rows:, :].astype(lower.dtype)
    for j in range(N_X):
        inner = lax.rem(x + j, N_X) * quarter
        keep_at = pl.multiple_of(core * half + inner, quarter)
        send_at = pl.multiple_of((1 - core) * half + inner, quarter)
        keep_out[j] = sums[:, pl.ds(keep_at, quarter), :]
        send_out[j] = sums[:, pl.ds(send_at, quarter), :]


def run_frames(place, counts, pos, obj, halos, pieces, amps, tables, iteration, middle):
    rows, cols = obj.shape[1], obj.shape[2]
    slots, size = amps.shape[1], amps.shape[2]
    vmem = pl.BlockSpec(memory_space=pltpu.VMEM)
    smem = pl.BlockSpec(memory_space=pltpu.SMEM)
    quarter = size // (N_CORE * N_X)
    if middle:
        shapes = [
            jax.ShapeDtypeStruct((2, rows + size, cols + size), F32),
            jax.ShapeDtypeStruct((2, rows + size, size), BF),
            jax.ShapeDtypeStruct((2, rows + size, size), BF),
        ]
    else:
        shapes = [
            jax.ShapeDtypeStruct((2, rows, cols), F32),
            jax.ShapeDtypeStruct((2, size, size), F32),
            jax.ShapeDtypeStruct((2, size, cols - size), BF),
            jax.ShapeDtypeStruct((2, rows, size), BF),
            jax.ShapeDtypeStruct((2, size, size), BF),
        ]
    shapes += [
        jax.ShapeDtypeStruct((N_X, 3, quarter, size), F32),
        jax.ShapeDtypeStruct((N_X, 3, quarter, size), F32),
        jax.ShapeDtypeStruct((1, 1), F32),
    ]
    scratch = [
        pltpu.VMEM((2, (cols + size) // LANES, rows + size, LANES), F32),
        pltpu.VMEM((2, (cols + size) // LANES, rows + size, LANES), F32),
        pltpu.VMEM((3, size, size), F32),
        pltpu.VMEM((GROUPS[0], 2 * size, size), BF),
        pltpu.VMEM((GROUPS[0], 2 * size, size), BF),
        pltpu.VMEM((GROUPS[0], 2, size, size), F32),
        pltpu.VMEM((slots, size, size), BF),
        pltpu.SemaphoreType.DMA((slots,)),
    ]
    lows, right, corner = halos
    scratch.append(pltpu.SemaphoreType.DMA((4 + len(lows) + len(pieces),)))
    scratch += [pltpu.VMEM(obj.shape, F32), pltpu.VMEM((2, size, cols), BF)]
    scratch += [pltpu.VMEM(value.shape, value.dtype) for value in (right, corner, *pieces, tables)]
    if len(pieces) > 1:
        scratch.append(pltpu.VMEM((2, size, size), F32))
    return pl.pallas_call(
        functools.partial(frames_kernel, middle, iteration, len(lows), len(pieces)),
        out_shape=shapes,
        in_specs=[smem] * 3 + [pl.BlockSpec(memory_space=pltpu.HBM)] * (5 + len(lows) + len(pieces)),
        out_specs=[vmem] * (len(shapes) - 1) + [smem],
        scratch_shapes=scratch,
        compiler_params=pltpu.CompilerParams(vmem_limit_bytes=46 << 20),
        cost_estimate=pl.CostEstimate(flops=6_000_000_000, bytes_accessed=8_000_000, transcendentals=0),
        name="frames",
    )(place, counts, pos, obj, *lows, right, corner, *pieces, amps, tables)


def spec(space):
    return pl.BlockSpec(memory_space=space)


def small_call(body, shapes, operands, name, limit=16):
    spaces = [pltpu.SMEM if v.size <= 2 else pltpu.VMEM for v in operands[0]] + [pl.ANY] * len(operands[1])
    return pl.pallas_call(
        body,
        out_shape=shapes,
        in_specs=[spec(space) for space in spaces],
        out_specs=[spec(pltpu.VMEM)] * len(shapes),
        compiler_params=pltpu.CompilerParams(vmem_limit_bytes=limit << 20),
        cost_estimate=pl.CostEstimate(flops=2_000_000, bytes_accessed=4_000_000, transcendentals=0),
        name=name,
    )(*operands[0], *operands[1])


def x_kernel(a, b, c, d, low_left, low_right, corner, total, down):
    size = low_left.shape[2]
    total[...] = a[0] + b[...] + c[...] + d[...]
    down[:, :, :size] = (low_left[...] + corner[...].astype(F32)).astype(BF)
    down[:, :, size:] = low_right[...]


def y_kernel(a, b, c, d, waited, total):
    total[...] = a[...] + b[...] + c[...] + d[...]


def probe_step(a, b, c, d, mine, fresh):
    total = a[...] + b[...] + c[...] + d[...]
    fresh[...] = mine[...] - total[:2] / (total[2:] + 1.0)


def z_kernel(a, b, c, d, mine, waited, fresh):
    probe_step(a, b, c, d, mine, fresh)


def object_step(obj, own, left, down, step, obj_out):
    size = left.shape[2]
    alpha = step[0, 0]
    obj_out[:, :, :size] = obj[:, :, :size] - alpha * (own[:, :, :size] + left[...].astype(F32))
    obj_out[:, :size, :size] -= alpha * down[:, :, :size].astype(F32)
    obj_out[:, :size, size:] = obj[:, :size, size:] - alpha * (own[:, :size, size:] + down[:, :, size:].astype(F32))
    obj_out[:, size:, size:] = obj[:, size:, size:] - alpha * own[:, size:, size:]


def last_kernel(obj, own, left, down, step, obj_out, done):
    object_step(obj, own, left, down, step, obj_out)
    done[...] = obj_out[0, :8, :LANES]


def stack_kernel(a, b, c, d, *rest):
    for j, chunk in enumerate((a, b, c, d)):
        rest[-1][j] = chunk[...]


def sum_kernel(a, b, c, d, *rest):
    total = rest[-1]
    total[...] = a[...].reshape(total.shape) + b[...] + c[...] + d[...]


def rim_kernel(a, b, c, d, grads, from_left, from_right, total, down, up):
    sum_kernel(a, b, c, d, total)
    size = down.shape[1]
    cols = grads.shape[2] - size
    rows = grads.shape[1] - size
    for out, span in ((down, slice(rows, rows + size)), (up, slice(0, size))):
        out[:, :, :size] = (grads[:, span, :size] + from_left[:, span].astype(F32)).astype(BF)
        out[:, :, size:cols] = grads[:, span, size:cols].astype(BF)
        out[:, :, cols:] = (grads[:, span, cols:] + from_right[:, span].astype(F32)).astype(BF)


def wide_kernel(
    obj, low_left, low_right, right, corner, grads, from_left, from_right, above, under, step,
    obj_out, below_out, right_out, corner_out,
):
    size = corner.shape[1]
    rows, cols = obj.shape[1], obj.shape[2]
    alpha = step[0, 0]
    for r in (slice(0, size), slice(size, rows), slice(rows, rows + size)):
        for c in (slice(0, size), slice(size, cols), slice(cols, cols + size)):
            outside_r, outside_c = r.start == rows, c.start == cols
            total = grads[:, r, c]
            if c.start == 0:
                total = total + from_left[:, r].astype(F32)
            if outside_c:
                total = total + from_right[:, r].astype(F32)
            if r.start == 0:
                total = total + above[:, :, c].astype(F32)
            if outside_r:
                total = total + under[:, :, c].astype(F32)
            if outside_r and outside_c:
                corner_out[...] = (corner[...].astype(F32) - alpha * total).astype(BF)
            elif outside_r:
                low = low_left if c.start == 0 else low_right
                below_out[:, :, c] = (low[...].astype(F32) - alpha * total).astype(BF)
            elif outside_c:
                right_out[:, r, :] = (right[:, r, :].astype(F32) - alpha * total).astype(BF)
            else:
                obj_out[:, r, c] = obj[:, r, c] - alpha * total


def probe_kernel(place, mine, other, out):
    core, x = place[0], place[1]
    size = out.shape[1]
    half, quarter = size // N_CORE, size // (N_CORE * N_X)
    for piece, side in ((mine, core), (other, 1 - core)):
        for j in range(N_X):
            at = pl.multiple_of(side * half + lax.rem(x - j + N_X, N_X) * quarter, quarter)
            out[:, pl.ds(at, quarter), :] = piece[j]


def moved(value, axis, count, steps):
    first, last = max(0, -steps), min(count, count - steps)
    return lax.ppermute(value, axis, [(s, s + steps) for s in range(first, last)])


def turned(value, axis, steps):
    return lax.ppermute(value, axis, [(s, (s + steps) % 4) for s in range(4)])


def swapped(value):
    return lax.ppermute(value, "core", [(0, 1), (1, 0)])


def halo(lows, right):
    size = right.shape[2]
    first = moved(lows[0], ROW, N_ROW, -1)
    right = moved(right, COL, N_COL, -1)
    others = [moved(low, ROW, N_ROW, -1) for low in lows[1:]]
    corner = moved(first[:, :, :size], COL, N_COL, -1)
    return ((first, *others), right, corner)


def around(value, axis):
    return [value] + [turned(value, axis, j) for j in (1, 2, 3)]


def local(tables, obj, probe, amps, positions, counts):
    rows, cols = obj.shape[1], obj.shape[2]
    size = probe.shape[-1]
    half, quarter = size // N_CORE, size // (N_CORE * N_X)
    core, x = lax.axis_index("core"), lax.axis_index("x")
    place = jnp.stack([core, x]).astype(jnp.int32)
    mine = lax.dynamic_slice(probe, (0, core * half + x * quarter, 0), (2, quarter, size))
    whole = jax.ShapeDtypeStruct(obj.shape, F32)
    flat = jax.ShapeDtypeStruct((2, size, cols), BF)
    tall = jax.ShapeDtypeStruct((2, rows, size), BF)
    share = jax.ShapeDtypeStruct((3, quarter, size), F32)
    part = jax.ShapeDtypeStruct(mine.shape, F32)
    lows = [obj[:, :size, :size].astype(BF), obj[:, :size, size:].astype(BF)]
    right = obj[:, :, :size].astype(BF)
    pieces = (probe,)
    row = jax.ShapeDtypeStruct((8, LANES), F32)
    half_probe = jax.ShapeDtypeStruct((N_X, *mine.shape), F32)
    halos = halo(lows, right)
    square = jax.ShapeDtypeStruct((2, size, size), BF)
    wide = jax.ShapeDtypeStruct((2, size, cols + size), BF)
    for iteration in range(ITERS):
        middle = iteration < ITERS - 1
        *grads, keep, send, step = run_frames(
            place, counts[iteration, 0], positions[iteration], obj, halos, pieces, amps, tables, iteration, middle
        )
        if middle:
            grads, to_right, to_left = grads
            from_left, from_right = moved(to_right, COL, N_COL, 1), moved(to_left, COL, N_COL, -1)
        else:
            own, low_left, low_right, right, corner = grads
            corner = moved(corner, COL, N_COL, 1)
            left = moved(right, COL, N_COL, 1)
        sums = keep + swapped(send)
        sums = [sums[:1]] + [turned(sums[j], "x", j) for j in (1, 2, 3)]
        if middle:
            (total,) = small_call(sum_kernel, [share], (sums, []), "x_sum")
            total, down, up = small_call(
                rim_kernel, [share, wide, wide], ([*around(total, "z"), grads, from_left, from_right], []), "z_sum_rims"
            )
            above, under = moved(down, ROW, N_ROW, 1), moved(up, ROW, N_ROW, -1)
            (mine,) = small_call(probe_step, [part], ([*around(total, "y"), mine], []), "y_sum")
            lows, right, corner = halos
            obj, below, right, corner = small_call(
                wide_kernel,
                [whole, flat, tall, square],
                ([obj, *lows, right, corner, grads, from_left, from_right, above, under, step], []),
                "wide_update",
                24,
            )
            halos, waited = ((below,), right, corner), [above, under]
        else:
            total, down = small_call(x_kernel, [share, flat], ([*sums, low_left, low_right, corner], []), "x_sum")
            down = moved(down, ROW, N_ROW, 1)
            (total,) = small_call(y_kernel, [share], (around(total, "y"), [left]), "y_sum")
            (mine,) = small_call(z_kernel, [part], ([*around(total, "z"), mine], [down]), "z_sum")
            obj, done = small_call(last_kernel, [whole, row], ([obj, own, left, down, step], []), "object_update")
            waited = [done]
        (stack,) = small_call(stack_kernel, [half_probe], (around(mine, "x"), waited), "half_probe")
        pieces = (stack, swapped(stack))
    shape = jax.ShapeDtypeStruct((2, size, size), F32)
    (probe,) = small_call(probe_kernel, [shape], ([place, *pieces], []), "probe_whole")
    return (obj, probe)


def solution(mesh):
    fine = Mesh(mesh.devices.reshape(N_X, N_Z, N_Y, N_CORE), ("x", "z", "y", "core"))
    placed = (
        P(None, ROW, COL),
        P(),
        P(None, ROW + COL, None, None),
        P(None, None, ROW + COL),
        P(None, COL, ROW),
    )
    blocks = jnp.asarray(chirp_blocks(256))
    return jax.shard_map(
        functools.partial(local, blocks),
        mesh=fine, in_specs=placed, out_specs=(P(None, ROW, COL), P()), check_vma=False,
    )
```

```python
import functools

import jax
import jax.numpy as jnp
import ml_dtypes
import numpy as np
from jax import lax
from jax.experimental import pallas as pl
from jax.experimental.pallas import tpu as pltpu
from jax.sharding import Mesh, PartitionSpec as P

ITERS = 2
FLOOR = 0.3
ALPHA = 0.5
LANES = 128
CHUNK = 32
GROUPS = (6, 2, 1)
N_X, N_Z, N_Y, N_CORE = 4, 4, 4, 2
N_ROW, N_COL = N_X * N_Z, N_Y * N_CORE
ROW, COL = ("x", "z"), ("y", "core")
BF, F32 = jnp.bfloat16, jnp.float32


def chirp_blocks(size):
    offset = np.arange(size, dtype=np.int64)
    units = (offset[:, None] - offset[None, :]) ** 2 % (2 * size)
    phase = np.float32(np.pi) * units.astype(np.float32) / np.float32(size)
    scale = np.float32(1.0 / np.sqrt(size))
    real = (np.cos(phase) * scale).astype(ml_dtypes.bfloat16)
    imag = (np.sin(phase) * scale).astype(ml_dtypes.bfloat16)
    forward = np.block([[real, -imag], [imag, real]])
    return np.stack([forward, forward.T])


def frames_kernel(
    middle, iteration, n_low, n_pieces,
    place, counts, pos, obj, *rest,
):
    lows, (right, corner), rest = rest[:n_low], rest[n_low : n_low + 2], rest[n_low + 2 :]
    pieces, (amps, tables), rest = rest[:n_pieces], rest[n_pieces : n_pieces + 2], rest[n_pieces + 2 :]
    n_grads = 3 if middle else 5
    grads_out, (keep_out, send_out, step_out) = rest[:n_grads], rest[n_grads : n_grads + 3]
    ext, acc, sums, wave, mis, patch, levels, arrived, here, *rest = rest[n_grads + 3 :]
    landing, probe_scratch = rest[: 5 + n_pieces], rest[5 + n_pieces :]
    count = counts[0]
    low_parts, at = [], 0
    for low in lows:
        low_parts.append(landing[1].at[:, :, at : at + low.shape[2]])
        at += low.shape[2]
    sources = (obj, right, corner, *lows, *pieces, tables)
    targets = (landing[0], *landing[2:4], *low_parts, *landing[4:])
    copies = [
        pltpu.make_async_copy(source, target, here.at[i])
        for i, (source, target) in enumerate(zip(sources, targets))
    ]
    for copy in copies:
        copy.start()
    obj, below, right, corner = landing[:4]
    pieces, tables = landing[4 : 4 + n_pieces], landing[4 + n_pieces]
    table_a, table_b = tables.at[0], tables.at[1]

    def fetch(index):
        return pltpu.make_async_copy(amps.at[iteration, index], levels.at[index], arrived.at[index])

    def begin(index, carry):
        fetch(index).start()
        return carry

    lax.fori_loop(0, count, begin, 0)
    rows, cols = obj.shape[1], obj.shape[2]
    size = corner.shape[1]
    row_chunks = size // CHUNK
    inner_tiles, all_tiles, left_tiles = cols // LANES, (cols + size) // LANES, size // LANES
    acc[...] = jnp.zeros_like(acc)
    sums[...] = jnp.zeros_like(sums)
    copies[0].wait()
    for copy in copies[1 : 3 + n_low]:
        copy.wait()
    for j in range(all_tiles):
        inside = j < inner_tiles
        at = (j if inside else j - inner_tiles) * LANES
        upper = obj if inside else right
        ext[:, j, :rows, :] = upper[:, :, at : at + LANES].astype(BF).astype(F32)
        lower = below if inside else corner
        ext[:, j, rows:, :] = lower[:, :, at : at + LANES].astype(F32)
    for copy in copies[3 + n_low :]:
        copy.wait()
    core, x = place[0], place[1]
    half, quarter = size // N_CORE, size // (N_CORE * N_X)
    if n_pieces == 1:
        (probe,) = pieces
    else:
        (probe,) = probe_scratch
        for piece, side in ((pieces[0], core), (pieces[1], 1 - core)):
            for j in range(N_X):
                at = pl.multiple_of(side * half + lax.rem(x - j + N_X, N_X) * quarter, quarter)
                probe[:, pl.ds(at, quarter), :] = piece[j]
    peak = jnp.max(probe[0] * probe[0] + probe[1] * probe[1])
    step_out[0, 0] = ALPHA / (peak + 1e-6)
    lane = lax.broadcasted_iota(jnp.int32, (CHUNK, LANES), 1)

    def frames(indices):
        work = []
        for index in indices:
            fetch(index).wait()
        for slot, index in enumerate(indices):
            top, left = pos[0, index], pos[1, index]
            base = left // LANES
            shift = left - base * LANES
            back_shift = lax.rem(LANES - shift, LANES)
            whole = lane < LANES - shift
            for k in range(row_chunks):
                span = slice(k * CHUNK, (k + 1) * CHUNK)
                parts = []
                for c in range(2):
                    tiles = [
                        pltpu.roll(ext[c, base + j, pl.ds(top + k * CHUNK, CHUNK), :], back_shift, 1)
                        for j in range(3)
                    ]
                    cut = jnp.concatenate(
                        [jnp.where(whole, tiles[0], tiles[1]), jnp.where(whole, tiles[1], tiles[2])], axis=1
                    )
                    patch[slot, c, span, :] = cut
                    parts.append(cut)
                re, im = parts
                pr, pi = probe[0, span, :], probe[1, span, :]
                wave[slot, span, :] = (pr * re - pi * im).astype(BF)
                wave[slot, size + k * CHUNK : size + (k + 1) * CHUNK, :] = (pr * im + pi * re).astype(BF)
                sums[2, span, :] += re * re + im * im
            work.append((index, top, base, shift))
        for slot, (index, top, base, shift) in enumerate(work):
            near = jnp.dot(table_a[...], wave[slot], preferred_element_type=F32).astype(BF)
            near = jnp.concatenate([near[:size], near[size:]], axis=1)
            far = jnp.dot(near, table_b[...], preferred_element_type=F32)
            fr, fi = far[:, :size], far[:, size:]
            scale = lax.rsqrt(jnp.maximum(fr * fr + fi * fi, FLOOR * FLOOR))
            factor = 1.0 - levels[index].astype(F32) * scale
            mis[slot, :size, :] = (fr * factor).astype(BF)
            mis[slot, size:, :] = (fi * factor).astype(BF)
        updates = []
        for slot, _ in enumerate(work):
            back = jnp.dot(table_b[...], mis[slot], preferred_element_type=F32).astype(BF)
            back = jnp.concatenate([back[:size], back[size:]], axis=1)
            updates.append(jnp.dot(back, table_a[...], preferred_element_type=F32))
        for slot, (index, top, base, shift) in enumerate(work):
            update = updates[slot]
            fresh = lane >= shift
            for k in range(row_chunks):
                span = slice(k * CHUNK, (k + 1) * CHUNK)
                ur, ui = update[span, :size], update[span, size:]
                pr, pi = probe[0, span, :], probe[1, span, :]
                re, im = patch[slot, 0, span, :], patch[slot, 1, span, :]
                sums[0, span, :] += re * ur + im * ui
                sums[1, span, :] += re * ui - im * ur
                grads = (pr * ur + pi * ui, pr * ui - pi * ur)
                for c in range(2):
                    grad = grads[c].astype(BF).astype(F32)
                    first = pltpu.roll(grad[:, :LANES], shift, 1)
                    second = pltpu.roll(grad[:, LANES:], shift, 1)
                    pieces = (
                        jnp.where(fresh, first, 0.0),
                        jnp.where(fresh, second, first),
                        jnp.where(fresh, 0.0, second),
                    )
                    for j, piece in enumerate(pieces):
                        acc[c, base + j, pl.ds(top + k * CHUNK, CHUNK), :] += piece

    done = 0
    for group in GROUPS:
        times = (count - done) // group

        def several(index, carry, first=done, group=group):
            frames([first + index * group + i for i in range(group)])
            return carry

        lax.fori_loop(0, times, several, 0)
        done = done + times * group
    if middle:
        all_out, to_right, to_left = grads_out
        for j in range(all_tiles):
            at = j * LANES
            all_out[:, :, at : at + LANES] = acc[:, j]
            if j < left_tiles:
                to_left[:, :, at : at + LANES] = acc[:, j].astype(BF)
            if j >= inner_tiles:
                at = at - cols
                to_right[:, :, at : at + LANES] = acc[:, j].astype(BF)
    else:
        own_out, low_left, low_right, right_out, corner_out = grads_out
        for j in range(all_tiles):
            inside = j < inner_tiles
            at = (j if inside else j - inner_tiles) * LANES
            upper = own_out if inside else right_out
            upper[:, :, at : at + LANES] = acc[:, j, :rows, :].astype(upper.dtype)
            lower = (low_left if j < left_tiles else low_right) if inside else corner_out
            at = at if j < left_tiles or not inside else at - size
            lower[:, :, at : at + LANES] = acc[:, j, rows:, :].astype(lower.dtype)
    for j in range(N_X):
        inner = lax.rem(x + j, N_X) * quarter
        keep_at = pl.multiple_of(core * half + inner, quarter)
        send_at = pl.multiple_of((1 - core) * half + inner, quarter)
        keep_out[j] = sums[:, pl.ds(keep_at, quarter), :]
        send_out[j] = sums[:, pl.ds(send_at, quarter), :]


def run_frames(place, counts, pos, obj, halos, pieces, amps, tables, iteration, middle):
    rows, cols = obj.shape[1], obj.shape[2]
    slots, size = amps.shape[1], amps.shape[2]
    vmem = pl.BlockSpec(memory_space=pltpu.VMEM)
    smem = pl.BlockSpec(memory_space=pltpu.SMEM)
    quarter = size // (N_CORE * N_X)
    if middle:
        shapes = [
            jax.ShapeDtypeStruct((2, rows + size, cols + size), F32),
            jax.ShapeDtypeStruct((2, rows + size, size), BF),
            jax.ShapeDtypeStruct((2, rows + size, size), BF),
        ]
    else:
        shapes = [
            jax.ShapeDtypeStruct((2, rows, cols), F32),
            jax.ShapeDtypeStruct((2, size, size), F32),
            jax.ShapeDtypeStruct((2, size, cols - size), BF),
            jax.ShapeDtypeStruct((2, rows, size), BF),
            jax.ShapeDtypeStruct((2, size, size), BF),
        ]
    shapes += [
        jax.ShapeDtypeStruct((N_X, 3, quarter, size), F32),
        jax.ShapeDtypeStruct((N_X, 3, quarter, size), F32),
        jax.ShapeDtypeStruct((1, 1), F32),
    ]
    scratch = [
        pltpu.VMEM((2, (cols + size) // LANES, rows + size, LANES), F32),
        pltpu.VMEM((2, (cols + size) // LANES, rows + size, LANES), F32),
        pltpu.VMEM((3, size, size), F32),
        pltpu.VMEM((GROUPS[0], 2 * size, size), BF),
        pltpu.VMEM((GROUPS[0], 2 * size, size), BF),
        pltpu.VMEM((GROUPS[0], 2, size, size), F32),
        pltpu.VMEM((slots, size, size), BF),
        pltpu.SemaphoreType.DMA((slots,)),
    ]
    lows, right, corner = halos
    scratch.append(pltpu.SemaphoreType.DMA((4 + len(lows) + len(pieces),)))
    scratch += [pltpu.VMEM(obj.shape, F32), pltpu.VMEM((2, size, cols), BF)]
    scratch += [pltpu.VMEM(value.shape, value.dtype) for value in (right, corner, *pieces, tables)]
    if len(pieces) > 1:
        scratch.append(pltpu.VMEM((2, size, size), F32))
    return pl.pallas_call(
        functools.partial(frames_kernel, middle, iteration, len(lows), len(pieces)),
        out_shape=shapes,
        in_specs=[smem] * 3 + [pl.BlockSpec(memory_space=pltpu.HBM)] * (5 + len(lows) + len(pieces)),
        out_specs=[vmem] * (len(shapes) - 1) + [smem],
        scratch_shapes=scratch,
        compiler_params=pltpu.CompilerParams(vmem_limit_bytes=46 << 20),
        cost_estimate=pl.CostEstimate(flops=6_000_000_000, bytes_accessed=8_000_000, transcendentals=0),
        name="frames",
    )(place, counts, pos, obj, *lows, right, corner, *pieces, amps, tables)


def spec(space):
    return pl.BlockSpec(memory_space=space)


def small_call(body, shapes, operands, name, limit=16):
    spaces = [pltpu.SMEM if v.size <= 2 else pltpu.VMEM for v in operands[0]] + [pl.ANY] * len(operands[1])
    return pl.pallas_call(
        body,
        out_shape=shapes,
        in_specs=[spec(space) for space in spaces],
        out_specs=[spec(pltpu.VMEM)] * len(shapes),
        compiler_params=pltpu.CompilerParams(vmem_limit_bytes=limit << 20),
        cost_estimate=pl.CostEstimate(flops=2_000_000, bytes_accessed=4_000_000, transcendentals=0),
        name=name,
    )(*operands[0], *operands[1])


def x_kernel(a, b, c, d, low_left, low_right, corner, total, down):
    size = low_left.shape[2]
    total[...] = a[0] + b[...] + c[...] + d[...]
    down[:, :, :size] = (low_left[...] + corner[...].astype(F32)).astype(BF)
    down[:, :, size:] = low_right[...]


def y_kernel(a, b, c, d, waited, total):
    total[...] = a[...] + b[...] + c[...] + d[...]


def probe_step(a, b, c, d, mine, fresh):
    total = a[...] + b[...] + c[...] + d[...]
    fresh[...] = mine[...] - total[:2] / (total[2:] + 1.0)


def z_kernel(a, b, c, d, mine, waited, fresh):
    probe_step(a, b, c, d, mine, fresh)


def object_step(obj, own, left, down, step, obj_out):
    size = left.shape[2]
    alpha = step[0, 0]
    obj_out[:, :, :size] = obj[:, :, :size] - alpha * (own[:, :, :size] + left[...].astype(F32))
    obj_out[:, :size, :size] -= alpha * down[:, :, :size].astype(F32)
    obj_out[:, :size, size:] = obj[:, :size, size:] - alpha * (own[:, :size, size:] + down[:, :, size:].astype(F32))
    obj_out[:, size:, size:] = obj[:, size:, size:] - alpha * own[:, size:, size:]


def strips_kernel(obj, low_left, low_right, right):
    size = right.shape[2]
    low_left[...] = obj[:, :size, :size].astype(BF)
    low_right[...] = obj[:, :size, size:].astype(BF)
    right[...] = obj[:, :, :size].astype(BF)


def last_kernel(obj, own, left, down, step, obj_out, done):
    object_step(obj, own, left, down, step, obj_out)
    done[...] = obj_out[0, :8, :LANES]


def stack_kernel(a, b, c, d, *rest):
    for j, chunk in enumerate((a, b, c, d)):
        rest[-1][j] = chunk[...]


def sum_kernel(a, b, c, d, *rest):
    total = rest[-1]
    total[...] = a[...].reshape(total.shape) + b[...] + c[...] + d[...]


def rim_kernel(a, b, c, d, grads, from_left, from_right, total, down, up):
    sum_kernel(a, b, c, d, total)
    size = down.shape[1]
    cols = grads.shape[2] - size
    rows = grads.shape[1] - size
    for out, span in ((down, slice(rows, rows + size)), (up, slice(0, size))):
        out[:, :, :size] = (grads[:, span, :size] + from_left[:, span].astype(F32)).astype(BF)
        out[:, :, size:cols] = grads[:, span, size:cols].astype(BF)
        out[:, :, cols:] = (grads[:, span, cols:] + from_right[:, span].astype(F32)).astype(BF)


def wide_kernel(
    obj, low_left, low_right, right, corner, grads, from_left, from_right, above, under, step,
    obj_out, below_out, right_out, corner_out,
):
    size = corner.shape[1]
    rows, cols = obj.shape[1], obj.shape[2]
    alpha = step[0, 0]
    for r in (slice(0, size), slice(size, rows), slice(rows, rows + size)):
        for c in (slice(0, size), slice(size, cols), slice(cols, cols + size)):
            outside_r, outside_c = r.start == rows, c.start == cols
            total = grads[:, r, c]
            if c.start == 0:
                total = total + from_left[:, r].astype(F32)
            if outside_c:
                total = total + from_right[:, r].astype(F32)
            if r.start == 0:
                total = total + above[:, :, c].astype(F32)
            if outside_r:
                total = total + under[:, :, c].astype(F32)
            if outside_r and outside_c:
                corner_out[...] = (corner[...].astype(F32) - alpha * total).astype(BF)
            elif outside_r:
                low = low_left if c.start == 0 else low_right
                below_out[:, :, c] = (low[...].astype(F32) - alpha * total).astype(BF)
            elif outside_c:
                right_out[:, r, :] = (right[:, r, :].astype(F32) - alpha * total).astype(BF)
            else:
                obj_out[:, r, c] = obj[:, r, c] - alpha * total


def probe_kernel(place, mine, other, out):
    core, x = place[0], place[1]
    size = out.shape[1]
    half, quarter = size // N_CORE, size // (N_CORE * N_X)
    for piece, side in ((mine, core), (other, 1 - core)):
        for j in range(N_X):
            at = pl.multiple_of(side * half + lax.rem(x - j + N_X, N_X) * quarter, quarter)
            out[:, pl.ds(at, quarter), :] = piece[j]


def moved(value, axis, count, steps):
    first, last = max(0, -steps), min(count, count - steps)
    return lax.ppermute(value, axis, [(s, s + steps) for s in range(first, last)])


def turned(value, axis, steps):
    return lax.ppermute(value, axis, [(s, (s + steps) % 4) for s in range(4)])


def swapped(value):
    return lax.ppermute(value, "core", [(0, 1), (1, 0)])


def halo(lows, right):
    size = right.shape[2]
    first = moved(lows[0], ROW, N_ROW, -1)
    right = moved(right, COL, N_COL, -1)
    others = [moved(low, ROW, N_ROW, -1) for low in lows[1:]]
    corner = moved(first[:, :, :size], COL, N_COL, -1)
    return ((first, *others), right, corner)


def around(value, axis):
    return [value] + [turned(value, axis, j) for j in (1, 2, 3)]


def local(tables, obj, probe, amps, positions, counts):
    rows, cols = obj.shape[1], obj.shape[2]
    size = probe.shape[-1]
    half, quarter = size // N_CORE, size // (N_CORE * N_X)
    core, x = lax.axis_index("core"), lax.axis_index("x")
    place = jnp.stack([core, x]).astype(jnp.int32)
    mine = lax.dynamic_slice(probe, (0, core * half + x * quarter, 0), (2, quarter, size))
    whole = jax.ShapeDtypeStruct(obj.shape, F32)
    flat = jax.ShapeDtypeStruct((2, size, cols), BF)
    tall = jax.ShapeDtypeStruct((2, rows, size), BF)
    share = jax.ShapeDtypeStruct((3, quarter, size), F32)
    part = jax.ShapeDtypeStruct(mine.shape, F32)
    square = jax.ShapeDtypeStruct((2, size, size), BF)
    narrow = jax.ShapeDtypeStruct((2, size, cols - size), BF)
    *lows, right = small_call(strips_kernel, [square, narrow, tall], ([obj], []), "strips")
    pieces = (probe,)
    row = jax.ShapeDtypeStruct((8, LANES), F32)
    half_probe = jax.ShapeDtypeStruct((N_X, *mine.shape), F32)
    halos = halo(lows, right)
    square = jax.ShapeDtypeStruct((2, size, size), BF)
    wide = jax.ShapeDtypeStruct((2, size, cols + size), BF)
    for iteration in range(ITERS):
        middle = iteration < ITERS - 1
        *grads, keep, send, step = run_frames(
            place, counts[iteration, 0], positions[iteration], obj, halos, pieces, amps, tables, iteration, middle
        )
        if middle:
            grads, to_right, to_left = grads
            from_left, from_right = moved(to_right, COL, N_COL, 1), moved(to_left, COL, N_COL, -1)
        else:
            own, low_left, low_right, right, corner = grads
            corner = moved(corner, COL, N_COL, 1)
            left = moved(right, COL, N_COL, 1)
        sums = keep + swapped(send)
        sums = [sums[:1]] + [turned(sums[j], "x", j) for j in (1, 2, 3)]
        if middle:
            (total,) = small_call(sum_kernel, [share], (sums, []), "x_sum")
            total, down, up = small_call(
                rim_kernel, [share, wide, wide], ([*around(total, "z"), grads, from_left, from_right], []), "z_sum_rims"
            )
            above, under = moved(down, ROW, N_ROW, 1), moved(up, ROW, N_ROW, -1)
            (mine,) = small_call(probe_step, [part], ([*around(total, "y"), mine], []), "y_sum")
            lows, right, corner = halos
            obj, below, right, corner = small_call(
                wide_kernel,
                [whole, flat, tall, square],
                ([obj, *lows, right, corner, grads, from_left, from_right, above, under, step], []),
                "wide_update",
                24,
            )
            halos, waited = ((below,), right, corner), [above, under]
        else:
            total, down = small_call(x_kernel, [share, flat], ([*sums, low_left, low_right, corner], []), "x_sum")
            down = moved(down, ROW, N_ROW, 1)
            (total,) = small_call(y_kernel, [share], (around(total, "y"), [left]), "y_sum")
            (mine,) = small_call(z_kernel, [part], ([*around(total, "z"), mine], [down]), "z_sum")
            obj, done = small_call(last_kernel, [whole, row], ([obj, own, left, down, step], []), "object_update")
            waited = [done]
        (stack,) = small_call(stack_kernel, [half_probe], (around(mine, "x"), waited), "half_probe")
        pieces = (stack, swapped(stack))
    shape = jax.ShapeDtypeStruct((2, size, size), F32)
    (probe,) = small_call(probe_kernel, [shape], ([place, *pieces], []), "probe_whole")
    return (obj, probe)


def solution(mesh):
    fine = Mesh(mesh.devices.reshape(N_X, N_Z, N_Y, N_CORE), ("x", "z", "y", "core"))
    placed = (
        P(None, ROW, COL),
        P(),
        P(None, ROW + COL, None, None),
        P(None, None, ROW + COL),
        P(None, COL, ROW),
    )
    blocks = jnp.asarray(chirp_blocks(256))
    return jax.shard_map(
        functools.partial(local, blocks),
        mesh=fine, in_specs=placed, out_specs=(P(None, ROW, COL), P()), check_vma=False,
    )
```
